32 devices in a mesh: gx: 4 (over y, x), gy: 8 (over z, core).
Axes of the slice: x: 2, y: 2, z: 4, core: 2. Of those that a mesh axis runs over, the one named last changes fastest.
Arguments:
- pressure: float32 [2, 512, 1024], P(None, 'gx', 'gy'), may hold values from 0.5 to 1.5
- saturations: float32 [2, 2, 512, 1024], P(None, None, 'gx', 'gy'), may hold values from 0.05 to 0.4
- old_mass: float32 [3, 2, 512, 1024], P(None, None, 'gx', 'gy'), may hold values from 0 to 0.4
- pore_volume: float32 [2, 512, 1024], P(None, 'gx', 'gy'), may hold values from 0.3 to 3
- transmissibility: float32 [3, 2, 512, 1024], P(None, None, 'gx', 'gy'), may hold values from 0.3 to 3
- direction: float32 [3, 2, 512, 1024], P(None, None, 'gx', 'gy'), may hold values from -6 to 6
- seg_pressure: float32 [128, 128], P('gx'), may hold values from 0.4 to 1.2
- seg_direction: float32 [128, 128], P('gx'), may hold values from -6 to 6
- perf_cell: int32 [128, 128], P('gx'), may hold values from 0 to 262143, as said below
- well_index: float32 [128, 128], P('gx'), may hold values from 0.2 to 2
- parent: int32 [128, 128], P('gx'), may hold values from 0 to 126, as said below
- seg_head: float32 [128, 128], P('gx'), may hold values from 0 to 0.3
- well_mode: int32 [128], P('gx'), may hold values from 0 to 1
- bhp_limit: float32 [128], P('gx'), may hold values from 0.3 to 0.8
- guide_rate: float32 [128], P('gx'), may hold values from 0.5 to 5
- group_of: int32 [128, 1], P('gx'), may hold values from 0 to 127
- group_target: float32 [128], replicated, may hold values from 200 to 800
Outputs:
- cell_residual: float32 [3, 2, 512, 1024], P(None, None, 'gx', 'gy')
- cell_jvp: float32 [3, 2, 512, 1024], P(None, None, 'gx', 'gy')
- seg_residual: float32 [128, 128], P(('gx', 'gy'))
- seg_jvp: float32 [128, 128], P(('gx', 'gy'))
- group_rates: float32 [3, 128], replicated
The draws below stay inside these ranges and needn't reach their ends.
Inputs may be any that keep to these rules, and one draw needn't show every extreme that they name: perf_cell codes (layer * 128 + xl) * 1024 + row, with xl the column within the strip of 128 columns of the well's block of 32 wells. `parent`: segment 0 of every well names itself; every other segment names a segment of lower number. `group_of`: every group has at least one well.
All inputs are finite; a program needn't handle non-finite values.
Results may differ from the reference program's by a relative error of at most 0.0003.
Values sent between devices are 32-bit elements; how exact they have to be, the bound alone decides.
No kernel may reach another device: no remote copies, remote signals or barrier semaphores. Data moves between devices by JAX's collectives and lax.ppermute only.
A program may use at most 128 MiB of HBM per device.

```python
import math
import jax
import jax.numpy as jnp
from jax import lax

NZ = 2
CX = 128
WELL_GX = 32
SEG = 128
GROUPS = 128
NX = 512
NY = 1024
WELLS = 128


def draw_perf_cell(key, part):
    keys = jax.random.split(jax.random.fold_in(key, 11), 5)
    head_col = jax.random.randint(keys[0], (WELLS, 1), 0, CX)
    head_row = jax.random.randint(keys[1], (WELLS, 1), 0, NY)
    column = jnp.clip(head_col + jax.random.randint(keys[2], (WELLS, SEG), -2, 3), 0, CX - 1)
    row_pos = jnp.clip(head_row + jax.random.randint(keys[3], (WELLS, SEG), -8, 9), 0, NY - 1)
    layer = jax.random.randint(keys[4], (WELLS, SEG), 0, NZ)
    coded = ((layer * CX + column) * NY + row_pos).astype(jnp.int32)
    coded = coded.at[WELLS - 1, SEG - 1].set(NZ * CX * NY - 1)
    coded = coded.at[0, 0].set(0)
    return coded


def draw_parent(key, part):
    upper = jnp.maximum(jnp.arange(SEG, dtype=jnp.int32), 1)
    chosen = jax.random.randint(jax.random.fold_in(key, 23), (WELLS, SEG), 0, upper[None, :])
    chosen = chosen.at[:, SEG - 1].set(SEG - 2)
    return chosen.astype(jnp.int32)


def place_ends(drawn, stream_key, least, largest):
    extent = drawn.shape
    place = [jax.random.randint(jax.random.fold_in(stream_key, axis), (), 0, extent[axis]) for axis in range(len(extent))]
    drawn = drawn.at[tuple(place)].set(least)
    longest = extent.index(max(extent))
    place[longest] = (place[longest] + 1) % extent[longest]
    return drawn.at[tuple(place)].set(largest)


def levels(own_key, shape, cuts, smallest, high):
    loudness, own = 1.0, jax.random.fold_in(own_key, 6)
    for dim, shards_of in cuts:
        steps = jnp.exp(jax.random.uniform(jax.random.fold_in(own, dim), (shards_of,), jnp.float32, smallest / len(cuts), high / len(cuts)))
        loudness = loudness * jnp.repeat(steps, shape[dim] // shards_of).reshape([-1 if axis == dim else 1 for axis in range(len(shape))])
    return loudness


def picks_of(rng, rows, amount, top, lift):
    order = jax.random.permutation(jax.random.fold_in(rng, 1), amount)
    favour = order
    for power in range(3):
        favour = favour * favour // amount
    favour = favour * lift // amount
    chance = jax.random.randint(jax.random.fold_in(rng, 2), (rows, amount), 0, 4096) + favour
    holders = jax.random.permutation(jax.random.fold_in(rng, 3), rows)[jnp.arange(amount) % rows]
    chance = jnp.where(jnp.arange(rows)[:, None] == holders[None, :], 1 << 14, chance)
    priority = chance * amount + jnp.arange(amount)
    return lax.top_k(priority.astype(jnp.int32), top)[1].astype(jnp.int32)


def bell_draw(key, shape, spread, limit, cuts=(), held_as=jnp.bfloat16):
    loudness = levels(key, shape, cuts, -0.22, 0.18) if cuts else 1.0
    drawn = jax.random.normal(key, shape, jnp.float32) * spread * loudness
    return jnp.minimum(jnp.maximum(drawn, -limit), limit).astype(held_as)


def setup_inputs(seed: int = 0) -> dict:
    splits = jax.random.split(jax.random.key(seed), 18)
    pressure = jnp.clip(0.5 + 1.0 * jax.random.uniform(splits[0], (NZ, NX, NY), jnp.float32) ** levels(splits[0], (NZ, NX, NY), ((1, 4), (2, 8)), -0.2, 0.2), 0.5, 1.5)
    saturations = jnp.clip(0.05 + 0.35 * jax.random.uniform(splits[1], (2, NZ, NX, NY), jnp.float32) ** levels(splits[1], (2, NZ, NX, NY), ((2, 4), (3, 8)), -0.2, 0.2), 0.05, 0.4)
    old_mass = jnp.clip(0.4 * jax.random.uniform(splits[2], (3, NZ, NX, NY), jnp.float32) ** levels(splits[2], (3, NZ, NX, NY), ((2, 4), (3, 8)), -0.2, 0.2), 0.0, 0.4)
    pore_volume = jnp.clip(jnp.exp(math.log(3.0) - 2.3025851 * jax.random.uniform(splits[3], (NZ, NX, NY), jnp.float32) ** levels(splits[3], (NZ, NX, NY), ((1, 4), (2, 8)), -0.2, 0.2)), 0.3, 3.0)
    transmissibility = jnp.clip(jnp.exp(math.log(3.0) - 2.3025851 * jax.random.uniform(splits[4], (3, NZ, NX, NY), jnp.float32) ** levels(splits[4], (3, NZ, NX, NY), ((2, 4), (3, 8)), -0.2, 0.2)), 0.3, 3.0)
    direction = bell_draw(splits[5], (3, NZ, NX, NY), 1.0, 6.0, ((2, 4), (3, 8)), jnp.float32)
    seg_pressure = jnp.clip(0.4 + 0.800000042 * jax.random.uniform(splits[6], (WELLS, SEG), jnp.float32) ** levels(splits[6], (WELLS, SEG), ((0, 4),), -0.2, 0.2), 0.4, 1.2)
    seg_direction = bell_draw(splits[7], (WELLS, SEG), 1.0, 6.0, ((0, 4),), jnp.float32)
    perf_cell = draw_perf_cell(jax.random.fold_in(splits[17], 71), 0)
    well_index = jnp.clip(jnp.exp(math.log(2.0) - 2.3025851 * jax.random.uniform(splits[9], (WELLS, SEG), jnp.float32) ** levels(splits[9], (WELLS, SEG), ((0, 4),), -0.2, 0.2)), 0.2, 2.0)
    parent = draw_parent(jax.random.fold_in(splits[17], 71), 0)
    seg_head = jnp.clip(0.3 * jax.random.uniform(splits[11], (WELLS, SEG), jnp.float32) ** levels(splits[11], (WELLS, SEG), ((0, 4),), -0.2, 0.2), 0.0, 0.3)
    well_mode = place_ends(jax.random.randint(splits[12], (WELLS,), 0, 2), jax.random.fold_in(splits[12], 1), 0, 1).astype(jnp.int32)
    bhp_limit = jnp.clip(0.3 + 0.5 * jax.random.uniform(splits[13], (WELLS,), jnp.float32) ** levels(splits[13], (WELLS,), ((0, 4),), -0.2, 0.2), 0.3, 0.8)
    guide_rate = jnp.clip(jnp.exp(math.log(5.0) - 2.3025851 * jax.random.uniform(splits[14], (WELLS,), jnp.float32) ** levels(splits[14], (WELLS,), ((0, 4),), -0.2, 0.2)), 0.5, 5.0)
    group_of = picks_of(splits[15], WELLS, GROUPS, 1, 64)
    group_target = jnp.clip(jax.random.uniform(splits[16], (GROUPS,), jnp.float32, 200.0, 800.0), 200.0, 800.0)
    return {"pressure": pressure, "saturations": saturations, "old_mass": old_mass, "pore_volume": pore_volume, "transmissibility": transmissibility, "direction": direction, "seg_pressure": seg_pressure, "seg_direction": seg_direction, "perf_cell": perf_cell, "well_index": well_index, "parent": parent, "seg_head": seg_head, "well_mode": well_mode, "bhp_limit": bhp_limit, "guide_rate": guide_rate, "group_of": group_of, "group_target": group_target}


COMPRESS = (0.05, 0.2, 1.0)
VISCOSITY = (0.5, 1.0, 0.2)
DENSITY = (1.0, 0.8, 0.2)
ROCK_COMP = 0.01
GRAVITY = 0.05
UPWIND_WIDTH = 0.02
FRICTION = 0.002
RATE_SCALE = 0.1


def phase_props(press, water, gas):
    oil = 1.0 - water - gas
    satur = (water, oil, gas)
    rock = 1.0 + ROCK_COMP * (press - 1.0)
    mobility = []
    masses = []
    for phase in range(3):
        volume = jnp.exp(COMPRESS[phase] * (press - 1.0))
        mobility.append(satur[phase] * satur[phase] * volume / VISCOSITY[phase])
        masses.append(rock * satur[phase] * volume)
    return jnp.stack(mobility), jnp.stack(masses)


def face_flux(press_in, press_out, mobil_in, mobil_out, trans, lift):
    fluxes = []
    for phase in range(3):
        potential = press_in - press_out + DENSITY[phase] * lift
        upwind = jax.nn.sigmoid(potential / UPWIND_WIDTH)
        fluxes.append(trans * (upwind * mobil_in[phase] + (1.0 - upwind) * mobil_out[phase]) * potential)
    return jnp.stack(fluxes)


def ancestry(parent):
    count = parent.shape[1]
    segment_ids = jnp.arange(count, dtype=jnp.int32)
    reach = (segment_ids[None, :, None] == segment_ids[None, None, :]) | (parent[:, None, :] == segment_ids[None, :, None])
    reach = reach.astype(jnp.float32)
    for level in range((count - 1).bit_length()):
        reach = jnp.minimum(jnp.einsum("wsu,wut->wst", reach, reach, precision=lax.Precision.HIGHEST), 1.0)
    return reach


def reference(pressure, saturations, old_mass, pore_volume, transmissibility, direction, seg_pressure, seg_direction, perf_cell, well_index, parent, seg_head, well_mode, bhp_limit, guide_rate, group_of, group_target):
    layer_span = CX * NY
    layer = perf_cell // layer_span
    remain = perf_cell % layer_span
    column = (jnp.arange(WELLS, dtype=jnp.int32) // WELL_GX)[:, None] * CX + remain // NY
    flat_cell = ((layer * NX + column) * NY + remain % NY).astype(jnp.int32)
    reach = ancestry(parent)
    member = (group_of[:, 0][:, None] == jnp.arange(GROUPS, dtype=jnp.int32)[None, :]).astype(jnp.float32)
    guide_total = jnp.dot(guide_rate, member, precision=lax.Precision.HIGHEST)
    target = jnp.dot(member, group_target, precision=lax.Precision.HIGHEST) * guide_rate / jnp.dot(member, guide_total, precision=lax.Precision.HIGHEST)

    def evaluate(press, satur, seg_press):
        mobility, masses = phase_props(press, satur[0], satur[1])
        residual = masses * pore_volume - old_mass
        flux_cols = face_flux(press[:, :-1], press[:, 1:], mobility[:, :, :-1], mobility[:, :, 1:], transmissibility[0][:, :-1], 0.0)
        residual = residual + jnp.pad(flux_cols, ((0, 0), (0, 0), (0, 1), (0, 0))) - jnp.pad(flux_cols, ((0, 0), (0, 0), (1, 0), (0, 0)))
        flux_rows = face_flux(press[:, :, :-1], press[:, :, 1:], mobility[:, :, :, :-1], mobility[:, :, :, 1:], transmissibility[1][:, :, :-1], 0.0)
        residual = residual + jnp.pad(flux_rows, ((0, 0), (0, 0), (0, 0), (0, 1))) - jnp.pad(flux_rows, ((0, 0), (0, 0), (0, 0), (1, 0)))
        flux_layers = face_flux(press[:-1], press[1:], mobility[:, :-1], mobility[:, 1:], transmissibility[2][:-1], GRAVITY)
        residual = residual + jnp.pad(flux_layers, ((0, 0), (0, 1), (0, 0), (0, 0))) - jnp.pad(flux_layers, ((0, 0), (1, 0), (0, 0), (0, 0)))
        mobil_flat = mobility.reshape(3, -1)
        rates = well_index * mobil_flat[:, flat_cell] * (press.reshape(-1)[flat_cell] - seg_press)
        residual = residual.reshape(3, -1).at[:, flat_cell.reshape(-1)].add(rates.reshape(3, -1)).reshape(residual.shape)
        flow = jnp.einsum("wst,wt->ws", reach, jnp.sum(rates, axis=0), precision=lax.Precision.HIGHEST)
        above = jnp.take_along_axis(seg_press, parent, axis=1)
        inner = seg_press - above - seg_head - FRICTION * flow
        root = jnp.where(well_mode == 1, RATE_SCALE * (flow[:, 0] - target), seg_press[:, 0] - bhp_limit)
        seg_res = inner.at[:, 0].set(root)
        return residual, seg_res, rates

    primal, tangent = jax.jvp(evaluate, (pressure, saturations, seg_pressure), (direction[0], direction[1:], seg_direction))
    cell_residual, seg_residual, rates = primal
    cell_jvp, seg_jvp, unused_rates = tangent
    group_rates = jnp.dot(jnp.sum(rates, axis=2), member, precision=lax.Precision.HIGHEST)
    return cell_residual, cell_jvp, seg_residual, seg_jvp, group_rates
```

```python
import functools

import jax
import jax.numpy as jnp
from jax import lax
from jax.experimental import pallas as pl
from jax.experimental.pallas import tpu as pltpu
from jax.sharding import PartitionSpec as P

COMPRESS = (0.05, 0.2, 1.0)
VISCOSITY = (0.5, 1.0, 0.2)
DENSITY = (1.0, 0.8, 0.2)
ROCK_COMP = 0.01
GRAVITY = 0.05
UPWIND_WIDTH = 0.02
FRICTION = 0.002
RATE_SCALE = 0.1

F32 = jnp.float32
BF16 = jnp.bfloat16
NN = (((1,), (0,)), ((), ()))
NT = (((1,), (1,)), ((), ()))


def dot(a, b, dims=NN):
    return lax.dot_general(a, b, dims, preferred_element_type=F32)


def iota(shape, dim):
    return lax.broadcasted_iota(jnp.int32, shape, dim)


def split(x, parts):
    terms = []
    for _ in range(parts):
        head = x.astype(BF16).astype(F32)
        terms.append(head)
        x = x - head
    return terms


def mobility_of(press, dpress, water, dwater, gas, dgas):
    satur = (water, 1.0 - water - gas, gas)
    dsatur = (dwater, -dwater - dgas, dgas)
    out = []
    for a in range(3):
        volume = jnp.exp(COMPRESS[a] * (press - 1.0))
        mass = satur[a] * volume
        cdp = COMPRESS[a] * dpress
        scaled = mass * (1.0 / VISCOSITY[a])
        mob = scaled * satur[a]
        dmob = scaled * (2.0 * dsatur[a] + satur[a] * cdp)
        dmass = volume * dsatur[a] + mass * cdp
        out.append((mob, dmob, mass, dmass))
    return out


def upwind_of(pot):
    return 0.5 * jnp.tanh(pot * (0.5 / UPWIND_WIDTH)) + 0.5


def face_terms(trans, pot, dpot):
    up = upwind_of(pot)
    dup = up * (1.0 - up) * (dpot * (1.0 / UPWIND_WIDTH))
    return up, dup, trans * pot, trans * dpot


def face_flux(terms, mob_in, dmob_in, mob_out, dmob_out):
    up, dup, tpot, tdpot = terms
    diff = mob_in - mob_out
    mob = mob_out + up * diff
    dmob = dmob_out + up * (dmob_in - dmob_out) + dup * diff
    return mob * tpot, dmob * tpot + mob * tdpot


def column_to_row(eye, column):
    return jnp.sum(jnp.where(eye, column, 0.0), axis=0, keepdims=True)


def located(code, all_rows, first_row):
    if all_rows & (all_rows - 1) == 0:
        lx = code >> (all_rows.bit_length() - 1)
        row = code & (all_rows - 1)
    else:
        lx = code // all_rows
        row = code - lx * all_rows
    return lx, row - first_row


def as_column(line):
    n = line.shape[1]
    diag = iota((n, n), 0) == iota((n, n), 1)
    return jnp.sum(jnp.where(diag, line, 0.0), axis=1, keepdims=True)


def list_wells(owned, active):
    wells = owned.shape[0]
    has = jnp.max(jnp.where(owned, 1.0, 0.0), axis=1, keepdims=True)
    count = jnp.int32(0)
    for part in range(0, wells, 16):
        size = min(16, wells - part)
        bit = (1 << iota((size, 1), 0)).astype(F32)
        bits = jnp.sum(has[part : part + size] * bit).astype(jnp.int32)
        for w in range(size):
            active[1 + count] = part + w
            count = count + ((bits >> w) & 1)
    active[0] = count
    for k in range(3):
        active[1 + count + k] = wells
    return count


def outer_flux(first, last, prev, after, has_prev, has_next, layers):
    def pick(x, q):
        return x[layers * q : layers * (q + 1)]

    ins = [jnp.concatenate([pick(prev, q), pick(last, q)], axis=0) for q in range(7)]
    outs = [jnp.concatenate([pick(first, q), pick(after, q)], axis=0) for q in range(6)]
    props = [mobility_of(*(x[q] for q in (0, 3, 1, 4, 2, 5))) for x in (ins, outs)]
    terms = face_terms(ins[6], ins[0] - outs[0], ins[3] - outs[3])
    fluxes = [
        face_flux(terms, props[0][a][0], props[0][a][1], props[1][a][0], props[1][a][1])
        for a in range(3)
    ]
    before = iota((2 * layers, first.shape[1]), 0) < layers
    valid = jnp.where(before, has_prev.astype(jnp.int32), has_next.astype(jnp.int32)) == 1
    return [jnp.where(valid, f, 0.0) for t in (0, 1) for f in (x[t] for x in fluxes)]


def wells_kernel(
    all_rows,
    perf_hbm,
    press_hbm,
    satur_hbm,
    direc_hbm,
    seg_p_hbm,
    seg_d_hbm,
    wi_hbm,
    guide_hbm,
    group_hbm,
    mode_hbm,
    bhp_hbm,
    group_target_hbm,
    trans_hbm,
    send,
    rates,
    rowloc,
    lxs,
    perf,
    press,
    satur,
    direc,
    seg_p,
    seg_d,
    wi,
    guide,
    group,
    mode,
    bhp,
    group_target,
    t_col,
    held,
    held_low,
    gath,
    active,
    sems,
):
    layers, cols, rows = press.shape
    cells = layers * cols
    wells, segs = seg_p.shape
    gx, gy = lax.axis_size("gx"), lax.axis_size("gy")
    xi, yi = lax.axis_index("gx"), lax.axis_index("gy")
    share = wells // gy
    moves = [
        pltpu.make_async_copy(src, dst, sems.at[k])
        for k, (src, dst) in enumerate(
            [
                (perf_hbm, perf),
                (press_hbm, press),
                (satur_hbm, satur),
                (direc_hbm, direc),
                (seg_p_hbm, seg_p),
                (seg_d_hbm, seg_d),
                (wi_hbm, wi),
                (guide_hbm, guide),
                (group_hbm, group),
                (mode_hbm, mode),
                (bhp_hbm, bhp),
                (group_target_hbm, group_target),
                (trans_hbm.at[0, :, pl.ds(cols - 8, 8), :], t_col),
            ]
        )
    ]
    for move in moves:
        move.start()

    moves[0].wait()
    lx_all, row_all = located(perf[...], all_rows, yi * rows)
    owned = (row_all >= 0) & (row_all < rows)
    nowhere = jnp.full((8, segs), -1, jnp.int32)
    lxs[0:wells, :] = lx_all
    rowloc[0:wells, :] = jnp.where(owned, row_all, -1)
    lxs[wells : wells + 8, :] = nowhere
    rowloc[wells : wells + 8, :] = nowhere
    count = list_wells(owned, active)

    for move in moves[4:]:
        move.wait()
    spot = iota((wells, 128), 1) - iota((wells, 128), 0)
    guides = jnp.where(spot == 3 * wells, as_column(guide[...]), 0.0)
    groups = jnp.where(spot == 0, as_column(group[...].astype(F32)), 0.0)
    groups = jnp.sum(groups, axis=0, keepdims=True)

    pick = iota((share, wells), 1) == iota((share, wells), 0) + yi * share

    def own(line):
        return jnp.sum(jnp.where(pick, line, 0.0), axis=1, keepdims=True)

    number = own(group[...].astype(F32))
    member = number == iota((share, 128), 1).astype(F32)
    columns = [
        own(mode[...].astype(F32)),
        own(guide[...]),
        number,
        jnp.sum(jnp.where(member, group_target[...], 0.0), axis=1, keepdims=True),
        own(bhp[...]),
    ]
    lane = iota((share, 128), 1)
    info = jnp.zeros((share, 128), F32)
    for k, column in enumerate(columns):
        info = jnp.where(lane == k, column, info)
    for q in range(6):
        rates[q, wells : wells + 8, :] = jnp.zeros((8, segs), F32)
    rates[0, wells + 4 : wells + 4 + share, :] = info

    edges = [[], []]
    fields = [press, satur.at[0], satur.at[1], direc.at[0], direc.at[1], direc.at[2]]
    arrive = {0: 1, 1: 2, 3: 3}
    for q, field in enumerate(fields):
        if q in arrive:
            moves[arrive[q]].wait()
        block = field[...].reshape(cells, rows)
        terms = split(block, 3 if q == 0 else 2)
        held[q, :, 0:rows] = terms[0].astype(BF16)
        held[q, :, rows : 2 * rows] = terms[1].astype(BF16)
        if q == 0:
            held_low[...] = terms[2].astype(BF16)
        for z in range(layers):
            edges[0].append(field[z, 0:1, :])
            edges[1].append(field[z, cols - 1 : cols, :])
    for z in range(layers):
        last = t_col[z, 7:8, :]
        edges[0].append(jnp.zeros_like(last))
        edges[1].append(last)
    chunk = send.shape[1]
    for side, step in ((0, -1), (1, 1)):
        there = xi + step
        edge = jnp.concatenate(edges[side], axis=0)

        @pl.when((there >= 0) & (there < gx))
        def _(edge=edge, to=there * gy + yi):
            send[pl.ds(to, 1), 0 : 7 * layers, :] = edge[None]

    def gather_wells(at, width):
        ids = [active[1 + at + k] for k in range(width)]
        row = jnp.concatenate([rowloc[pl.ds(w, 1), :] for w in ids], axis=1)
        lx = jnp.concatenate([lxs[pl.ds(w, 1), :] for w in ids], axis=1)
        hot = jnp.where(iota((rows, width * segs), 0) == row, 1.0, 0.0).astype(BF16)
        hot2 = jnp.concatenate([hot, hot], axis=0)
        here = iota((cells, width * segs), 0) == lx
        for q in range(len(fields)):
            found = dot(held[q], hot2)
            if q == 0:
                found = found + dot(held_low[...], hot)
            line = jnp.sum(jnp.where(here, found, 0.0), axis=0, keepdims=True)
            for k, w in enumerate(ids):
                gath[q, pl.ds(w, 1), :] = line[:, k * segs : (k + 1) * segs]

    def gather_step(i, carry):
        gather_wells(4 * i, 4)
        return carry

    fours = (count + 1) // 4
    lax.fori_loop(0, fours, gather_step, 0)

    @pl.when(count > 4 * fours)
    def _():
        gather_wells(4 * fours, 2)

    vals = [gath[q, 0:wells, :] for q in range(len(fields))]
    props = mobility_of(vals[0], vals[3], vals[1], vals[4], vals[2], vals[5])
    drop = vals[0] - seg_p[...]
    ddrop = vals[3] - seg_d[...]
    weight = wi[...]
    total = jnp.zeros((wells, segs), F32)
    dtotal = jnp.zeros((wells, segs), F32)
    line = guides
    for a in range(3):
        mob, dmob = props[a][0], props[a][1]
        rate = jnp.where(owned, weight * mob * drop, 0.0)
        drate = jnp.where(owned, weight * (dmob * drop + mob * ddrop), 0.0)
        total = total + rate
        dtotal = dtotal + drate
        rates[a, 0:wells, :] = rate
        rates[3 + a, 0:wells, :] = drate
        of_well = jnp.sum(rate, axis=1, keepdims=True)
        line = jnp.where(spot == a * wells, of_well, line)
    line = jnp.sum(line, axis=0, keepdims=True)
    lines = jnp.concatenate([line, groups], axis=0)
    for y in range(gy):
        both = jnp.concatenate(
            [total[y * share : (y + 1) * share], dtotal[y * share : (y + 1) * share]], axis=0
        )
        send[pl.ds(xi * gy + y, 1), 0 : 2 * share, :] = both[None]
    for to in range(gx * gy):
        send[to, chunk - 2 : chunk, :] = lines


def cells_kernel(
    press,
    satur,
    pore,
    trans,
    direc,
    parent,
    seg_p,
    seg_d,
    head,
    inner,
    reach,
    known,
    edges,
    inside_pair,
    between_pairs,
    mobs,
    base,
):
    layers, cols, rows = press.shape
    chunks = cols // 8
    wells, segs = seg_p.shape
    share = reach.shape[0]
    start = lax.axis_index("gy") * share

    eye = iota((cols, rows), 0) == iota((cols, rows), 1)
    fields = [press, satur.at[0], satur.at[1], direc.at[0], direc.at[1], direc.at[2]]
    for side in range(4):
        lines = fields + [trans.at[side // 2]]
        for q, field in enumerate(lines):
            for z in range(layers):
                if q == 6 and side % 2 == 0:
                    line = jnp.zeros((1, rows), F32)
                elif side < 2:
                    line = field[z, 0:1, :] if side == 0 else field[z, cols - 1 : cols, :]
                else:
                    at = 0 if side == 2 else rows - 1
                    line = column_to_row(eye, field[z, :, at : at + 1])
                edges[side, q * layers + z : q * layers + z + 1, :] = line
    even = lax.rem(lax.axis_index("gy"), 2) == 0
    inside_pair[...] = jnp.where(even, edges[3], edges[2])
    between_pairs[...] = jnp.where(even, edges[2], edges[3])

    sub, lane = iota((segs, segs), 0), iota((segs, segs), 1)
    pad = jnp.zeros((10, segs), F32)
    mine = pl.ds(start, share)
    p_own, d_own = seg_p[mine, :], seg_d[mine, :]
    reaches, aboves, daboves = [], [], []
    for i in range(share):
        link = sub == parent[pl.ds(start + i, 1), :]
        reaches.append(jnp.where(link | (sub == lane), 1.0, 0.0).astype(BF16))
        lines = split(p_own[i : i + 1], 3) + split(d_own[i : i + 1], 3) + [pad]
        lines = jnp.concatenate(lines, axis=0).astype(BF16)
        found = dot(lines, jnp.where(link, 1.0, 0.0).astype(BF16))
        aboves.append(found[0:1] + found[1:2] + found[2:3])
        daboves.append(found[3:4] + found[4:5] + found[5:6])
    above, dabove = jnp.concatenate(aboves, axis=0), jnp.concatenate(daboves, axis=0)
    first = iota((share, segs), 1) == 0
    known[0:share, :] = jnp.where(first, p_own, p_own - above - head[mine, :])
    known[share : 2 * share, :] = jnp.where(first, d_own, d_own - dabove)

    for c in range(chunks):
        at = slice(8 * c, 8 * c + 8)
        for z in range(layers):
            p, dp = press[z, at, :], direc[0, z, at, :]
            props = mobility_of(
                p, dp, satur[0, z, at, :], direc[1, z, at, :], satur[1, z, at, :], direc[2, z, at, :]
            )
            rock = 1.0 + ROCK_COMP * (p - 1.0)
            drock = ROCK_COMP * dp
            pv = pore[z, at, :]
            for a in range(3):
                mob, dmob, mass, dmass = props[a]
                mobs[a, z, at, :] = mob
                mobs[3 + a, z, at, :] = dmob
                base[a, z, at, :] = pv * (rock * mass)
                base[3 + a, z, at, :] = pv * (drock * mass + rock * dmass)

    sub = iota((8, rows), 0)
    lane = iota((8, rows), 1)
    levels = (segs - 1).bit_length()
    refs = [press, direc.at[0]] + [mobs.at[k] for k in range(6)]

    def load(c):
        held = [[ref[z, 8 * c : 8 * c + 8, :] for ref in refs] for z in range(layers)]
        return held, [[pltpu.roll(x, 7, 0) for x in line] for line in held]

    before = [[jnp.zeros((8, rows), F32)] * layers for _ in range(6)]
    now, up = load(0)
    for c in range(chunks):
        at = slice(8 * c, 8 * c + 8)
        last_chunk = c == chunks - 1
        if not last_chunk:
            later, up_later = load(c + 1)
        sums = []
        for z in range(layers):
            if last_chunk:
                nexts = up[z]
            else:
                nexts = [jnp.where(sub == 7, x, y) for x, y in zip(up_later[z], up[z])]
            sides = [pltpu.roll(x, rows - 1, 1) for x in now[z]]
            p, dp = now[z][0:2]
            t_col, t_row = trans[0, z, at, :], trans[1, z, at, :]
            if last_chunk:
                t_col = jnp.where(sub == 7, 0.0, t_col)
            t_row = jnp.where(lane == rows - 1, 0.0, t_row)
            col = face_terms(t_col, p - nexts[0], dp - nexts[1])
            row = face_terms(t_row, p - sides[0], dp - sides[1])
            divergence = []
            for a in range(3):
                m, dm = now[z][2 + a], now[z][5 + a]
                flux_col = face_flux(col, m, dm, nexts[2 + a], nexts[5 + a])
                flux_row = face_flux(row, m, dm, sides[2 + a], sides[5 + a])
                both = []
                for t in (0, 1):
                    f, g = flux_col[t], flux_row[t]
                    rolled = pltpu.roll(f, 1, 0)
                    down = jnp.where(sub == 0, before[3 * t + a][z], rolled)
                    before[3 * t + a][z] = rolled
                    both.append(base[3 * t + a, z, at, :] + (f - down) + (g - pltpu.roll(g, 1, 1)))
                divergence.append(both)
            sums.append(divergence)
        for z in range(layers - 1):
            dpot = now[z][1] - now[z + 1][1]
            t_lay = trans[2, z, at, :]
            for a in range(3):
                pot = now[z][0] - now[z + 1][0] + DENSITY[a] * GRAVITY
                terms = face_terms(t_lay, pot, dpot)
                flux = face_flux(
                    terms, now[z][2 + a], now[z][5 + a], now[z + 1][2 + a], now[z + 1][5 + a]
                )
                for t in (0, 1):
                    sums[z][a][t] = sums[z][a][t] + flux[t]
                    sums[z + 1][a][t] = sums[z + 1][a][t] - flux[t]
        for z in range(layers):
            for a in range(3):
                for t in (0, 1):
                    inner[3 * t + a, z, at, :] = sums[z][a][t]
        if not last_chunk:
            now, up = later, up_later
        if c % 2 == 1 and c // 2 < levels:
            for i in range(share):
                reaches[i] = jnp.minimum(dot(reaches[i], reaches[i]), 1.0).astype(BF16)
    for level in range(chunks // 2, levels):
        for i in range(share):
            reaches[i] = jnp.minimum(dot(reaches[i], reaches[i]), 1.0).astype(BF16)
    for i in range(share):
        reach[i] = reaches[i]


def scatter_kernel(
    inner,
    old_mass,
    rates,
    rowloc,
    lxs,
    acc,
    packed,
    active,
):
    layers, cols, rows = acc.shape[1:]
    cells = layers * cols
    wells, segs = rates.shape[1] - 8, rates.shape[2]
    count = list_wells(rowloc[0:wells, :] >= 0, active)
    packed[...] = rates[0, wells + 4 : wells + 4 + packed.shape[0], :]

    for k in range(6):
        acc[k] = inner[k] - old_mass[k] if k < 3 else inner[k]

    sub_row = iota((rows, 4 * segs), 0)
    sub_lx = iota((cells, 4 * segs), 0)

    def scatter_wells(i, carry):
        ids = [active[1 + 4 * i + k] for k in range(4)]
        row = jnp.concatenate([rowloc[pl.ds(w, 1), :] for w in ids], axis=1)
        lx = jnp.concatenate([lxs[pl.ds(w, 1), :] for w in ids], axis=1)
        at = sub_row == row
        hot = jnp.where(sub_lx == lx, 1.0, 0.0).astype(BF16)
        hot = jnp.concatenate([hot, hot], axis=1)
        for q in range(0, 6, 2):
            both = []
            for k in (q, q + 1):
                rate = jnp.concatenate([rates[k, pl.ds(w, 1), :] for w in ids], axis=1)
                terms = [jnp.where(at, term, 0.0).astype(BF16) for term in split(rate, 2)]
                both.append(jnp.concatenate(terms, axis=1))
            part = dot(hot, jnp.concatenate(both, axis=0), NT)
            acc[q] = acc[q] + part[:, 0:rows].reshape(layers, cols, rows)
            acc[q + 1] = acc[q + 1] + part[:, rows : 2 * rows].reshape(layers, cols, rows)
        return carry

    lax.fori_loop(0, (count + 3) // 4, scatter_wells, 0)


def sides_kernel(
    acc, edges, inside_pair, between_pairs, out_hbm, dout_hbm, rims, out, turned, sems
):
    layers, cols, rows = out.shape[1:]
    gy, yi = lax.axis_size("gy"), lax.axis_index("gy")
    even = lax.rem(yi, 2) == 0
    one, other = inside_pair[...], between_pairs[...]
    prev, after = jnp.where(even, other, one), jnp.where(even, one, other)
    flux = outer_flux(edges[2], edges[3], prev, after, yi > 0, yi < gy - 1, layers)
    spare = jnp.zeros((128 - 12 * layers, rows), F32)
    turned[...] = jnp.concatenate(flux + [spare], axis=0).T
    lane = iota((cols, rows), 1)
    moves = []
    for k in range(6):
        for z in range(layers):
            j = 2 * layers * k + z
            before = turned[:, j : j + 1]
            behind = turned[:, j + layers : j + layers + 1]
            side = jnp.where(lane == 0, -before, jnp.where(lane == rows - 1, behind, 0.0))
            out[k, z] = acc[k, z] + side
            rims[k, 0, z] = out[k, z, 0:8, :]
            rims[k, 1, z] = out[k, z, cols - 8 : cols, :]
        final = out_hbm.at[k] if k < 3 else dout_hbm.at[k - 3]
        moves.append(pltpu.make_async_copy(out.at[k], final, sems.at[k]))
        moves[k].start()
    for move in moves:
        move.wait()


def finish_kernel(
    wells,
    out_before,
    dout_before,
    rims,
    reach,
    known,
    packed,
    edges,
    got,
    out_hbm,
    dout_hbm,
    seg_out_hbm,
    seg_dout_hbm,
    group_out_hbm,
    tiles,
    seg_out,
    seg_dout,
    group_out,
    sems,
):
    del out_before, dout_before
    layers = tiles.shape[3]
    cols = out_hbm.shape[2]
    share, segs = seg_out.shape
    gx, gy = lax.axis_size("gx"), lax.axis_size("gy")
    xi, yi = lax.axis_index("gx"), lax.axis_index("gy")
    chunk = got.shape[1]

    has_prev, has_next = xi > 0, xi < gx - 1
    prev, after = (
        got[pl.ds(jnp.where(inside, x * gy + yi, 0), 1), 0 : 7 * layers, :][0]
        for inside, x in ((has_prev, xi - 1), (has_next, xi + 1))
    )
    flux = outer_flux(edges[0], edges[1], prev, after, has_prev, has_next, layers)
    moves = []

    def write(src, dst):
        move = pltpu.make_async_copy(src, dst, sems.at[len(moves)])
        move.start()
        moves.append(move)

    for t, final in ((0, out_hbm), (1, dout_hbm)):
        for side, at in ((0, 0), (1, 7)):
            for a in range(3):
                k = 3 * t + a
                for z in range(layers):
                    tiles[t, side, a, z] = rims[k, side, z]
                    f = flux[k][side * layers + z : side * layers + z + 1]
                    line = rims[k, side, z, at : at + 1, :]
                    tiles[t, side, a, z, at : at + 1, :] = line - f if side == 0 else line + f
            write(tiles.at[t, side], final.at[:, :, pl.ds(side * (cols - 8), 8), :])

    total = got[xi * gy, 0 : 2 * share, :]
    for y in range(1, gy):
        total = total + got[xi * gy + y, 0 : 2 * share, :]

    lines, numbers = [], []
    for x in range(gx):
        line = got[x * gy, chunk - 2 : chunk - 1, :]
        more = line
        for y in range(1, gy):
            more = more + got[x * gy + y, chunk - 2 : chunk - 1, :]
        lines.append(jnp.where(iota((1, 128), 1) < 3 * wells, more, line))
        numbers.append(got[x * gy, chunk - 1 : chunk, :])
    columns = jnp.concatenate(lines + numbers + [jnp.zeros((128 - 2 * gx, 128), F32)], axis=0).T
    group_sums = [jnp.zeros((wells, 128), F32)] * 4
    for x in range(gx):
        member = columns[0:wells, gx + x : gx + x + 1] == iota((wells, 128), 1).astype(F32)
        for a in range(4):
            values = columns[a * wells : (a + 1) * wells, x : x + 1]
            group_sums[a] = group_sums[a] + jnp.where(member, values, 0.0)
    for a in range(3):
        group_out[a : a + 1, :] = jnp.sum(group_sums[a], axis=0, keepdims=True)
    write(group_out, group_out_hbm)
    guide_total = jnp.sum(group_sums[3], axis=0, keepdims=True)

    flows, dflows = [], []
    pad = jnp.zeros((10, segs), F32)
    for i in range(share):
        lines = split(total[i : i + 1], 3) + split(total[share + i : share + i + 1], 3) + [pad]
        flow = dot(jnp.concatenate(lines, axis=0).astype(BF16), reach[i], NT)
        flows.append(flow[0:1] + flow[1:2] + flow[2:3])
        dflows.append(flow[3:4] + flow[4:5] + flow[5:6])
    flow, dflow = jnp.concatenate(flows, axis=0), jnp.concatenate(dflows, axis=0)
    column = [packed[:, k : k + 1] for k in range(5)]
    member = column[2] == iota((share, 128), 1).astype(F32)
    of_group = jnp.sum(jnp.where(member, guide_total, 0.0), axis=1, keepdims=True)
    target = column[3] * column[1] / of_group
    by_rate = column[0] == 1.0
    first = iota((share, segs), 1) == 0
    limit, dlimit = known[0:share, :], known[share : 2 * share, :]
    root = jnp.where(by_rate, RATE_SCALE * (flow - target), limit - column[4])
    droot = jnp.where(by_rate, RATE_SCALE * dflow, dlimit)
    seg_out[...] = jnp.where(first, root, limit - FRICTION * flow)
    seg_dout[...] = jnp.where(first, droot, dlimit - FRICTION * dflow)
    write(seg_out, seg_out_hbm)
    write(seg_dout, seg_dout_hbm)
    for move in moves:
        move.wait()


VMEM = pl.BlockSpec(memory_space=pltpu.VMEM)
ANY = pl.BlockSpec(memory_space=pl.ANY)


def params(mebibytes):
    return pltpu.CompilerParams(vmem_limit_bytes=mebibytes * 1024 * 1024)


def per_device(
    pressure,
    saturations,
    old_mass,
    pore_volume,
    transmissibility,
    direction,
    seg_pressure,
    seg_direction,
    perf_cell,
    well_index,
    parent,
    seg_head,
    well_mode,
    bhp_limit,
    guide_rate,
    group_of,
    group_target,
):
    layers, cols, rows = pressure.shape
    wells, segs = seg_pressure.shape
    cells = layers * cols
    gx, gy = lax.axis_size("gx"), lax.axis_size("gy")
    share = wells // gy
    edge_rows = 7 * layers
    chunk = 2 + max(2 * share, edge_rows)
    shape = jax.ShapeDtypeStruct

    guide_line = guide_rate.reshape(1, wells)
    group_line = group_of.reshape(1, wells)
    send, rates, rowloc, lxs = pl.pallas_call(
        functools.partial(wells_kernel, rows * gy),
        out_shape=(
            shape((gx * gy, chunk, 128), F32),
            shape((6, wells + 8, segs), F32),
            shape((wells + 8, segs), jnp.int32),
            shape((wells + 8, segs), jnp.int32),
        ),
        in_specs=[ANY] * 13,
        out_specs=(VMEM,) * 4,
        scratch_shapes=[
            pltpu.VMEM((wells, segs), jnp.int32),
            pltpu.VMEM((layers, cols, rows), F32),
            pltpu.VMEM((2, layers, cols, rows), F32),
            pltpu.VMEM((3, layers, cols, rows), F32),
            pltpu.VMEM((wells, segs), F32),
            pltpu.VMEM((wells, segs), F32),
            pltpu.VMEM((wells, segs), F32),
            pltpu.VMEM((1, wells), F32),
            pltpu.VMEM((1, wells), jnp.int32),
            pltpu.VMEM((1, wells), jnp.int32),
            pltpu.VMEM((1, wells), F32),
            pltpu.VMEM((1, 128), F32),
            pltpu.VMEM((layers, 8, rows), F32),
            pltpu.VMEM((6, cells, 2 * rows), BF16),
            pltpu.VMEM((cells, rows), BF16),
            pltpu.VMEM((6, wells + 8, segs), F32),
            pltpu.SMEM((wells + 8,), jnp.int32),
            pltpu.SemaphoreType.DMA((13,)),
        ],
        compiler_params=params(56),
        name="wells",
    )(
        perf_cell,
        pressure,
        saturations,
        direction,
        seg_pressure,
        seg_direction,
        well_index,
        guide_line,
        group_line,
        well_mode.reshape(1, wells),
        bhp_limit.reshape(1, wells),
        group_target.reshape(1, 128),
        transmissibility,
    )

    got = lax.all_to_all(send, ("gx", "gy"), 0, 0, tiled=True)

    seg_head, rowloc = lax.optimization_barrier((seg_head, rowloc))

    inner, reach, known, edges, inside_pair, between_pairs = pl.pallas_call(
        cells_kernel,
        out_shape=(
            shape((6, layers, cols, rows), F32),
            shape((share, segs, segs), BF16),
            shape((2 * share, segs), F32),
            shape((4, edge_rows, 128), F32),
            shape((edge_rows, 128), F32),
            shape((edge_rows, 128), F32),
        ),
        in_specs=[VMEM] * 9,
        out_specs=(VMEM,) * 6,
        scratch_shapes=[
            pltpu.VMEM((6, layers, cols, rows), F32),
            pltpu.VMEM((6, layers, cols, rows), F32),
        ],
        compiler_params=params(32),
        cost_estimate=pl.CostEstimate(flops=300_000_000, bytes_accessed=4_000_000, transcendentals=400_000),
        name="cells",
    )(
        pressure,
        saturations,
        pore_volume,
        transmissibility,
        direction,
        parent,
        seg_pressure,
        seg_direction,
        seg_head,
    )

    def swap(x, first):
        pairs = [(i, i + 1) for i in range(first, gy - 1, 2)]
        return lax.ppermute(x, "gy", pairs + [(j, i) for i, j in pairs])

    inside_pair = swap(inside_pair, 0)
    between_pairs = swap(between_pairs, 1)

    cell_shape = shape((3, layers, cols, rows), F32)
    summed, packed = pl.pallas_call(
        scatter_kernel,
        out_shape=(shape((6, layers, cols, rows), F32), shape((share, 128), F32)),
        in_specs=[VMEM] * 5,
        out_specs=(VMEM, VMEM),
        scratch_shapes=[pltpu.SMEM((wells + 8,), jnp.int32)],
        compiler_params=params(32),
        cost_estimate=pl.CostEstimate(flops=300_000_000, bytes_accessed=4_000_000, transcendentals=0),
        name="scatter",
    )(
        inner,
        old_mass,
        rates,
        rowloc,
        lxs,
    )

    out, dout, rims = pl.pallas_call(
        sides_kernel,
        out_shape=(cell_shape, cell_shape, shape((6, 2, layers, 8, rows), F32)),
        in_specs=[VMEM] * 4,
        out_specs=(ANY, ANY, VMEM),
        scratch_shapes=[
            pltpu.VMEM((6, layers, cols, rows), F32),
            pltpu.VMEM((cols, 128), F32),
            pltpu.SemaphoreType.DMA((6,)),
        ],
        compiler_params=params(32),
        cost_estimate=pl.CostEstimate(flops=3_000_000, bytes_accessed=4_000_000, transcendentals=10_000),
        name="sides",
    )(summed, edges, inside_pair, between_pairs)

    out, dout, seg_out, seg_dout, groups = pl.pallas_call(
        functools.partial(finish_kernel, wells),
        out_shape=(
            cell_shape,
            cell_shape,
            shape((share, segs), F32),
            shape((share, segs), F32),
            shape((3, 128), F32),
        ),
        in_specs=[ANY] * 2 + [VMEM] * 6,
        out_specs=(ANY,) * 5,
        input_output_aliases={0: 0, 1: 1},
        scratch_shapes=[
            pltpu.VMEM((2, 2, 3, layers, 8, rows), F32),
            pltpu.VMEM((share, segs), F32),
            pltpu.VMEM((share, segs), F32),
            pltpu.VMEM((3, 128), F32),
            pltpu.SemaphoreType.DMA((7,)),
        ],
        compiler_params=params(32),
        name="finish",
    )(out, dout, rims, reach, known, packed, edges, got)
    return out, dout, seg_out, seg_dout, groups


def solution(mesh):
    placed = (
        P(None, "gx", "gy"),
        P(None, None, "gx", "gy"),
        P(None, None, "gx", "gy"),
        P(None, "gx", "gy"),
        P(None, None, "gx", "gy"),
        P(None, None, "gx", "gy"),
        P("gx", None),
        P("gx", None),
        P("gx", None),
        P("gx", None),
        P("gx", None),
        P("gx", None),
        P("gx"),
        P("gx"),
        P("gx"),
        P("gx", None),
        P(),
    )
    return jax.shard_map(
        per_device,
        mesh=mesh,
        in_specs=placed,
        out_specs=(
            P(None, None, "gx", "gy"),
            P(None, None, "gx", "gy"),
            P(("gx", "gy"), None),
            P(("gx", "gy"), None),
            P(),
        ),
        check_vma=False,
    )
```

```python
import functools

import jax
import jax.numpy as jnp
from jax import lax
from jax.experimental import pallas as pl
from jax.experimental.pallas import tpu as pltpu
from jax.sharding import PartitionSpec as P

COMPRESS = (0.05, 0.2, 1.0)
VISCOSITY = (0.5, 1.0, 0.2)
DENSITY = (1.0, 0.8, 0.2)
ROCK_COMP = 0.01
GRAVITY = 0.05
UPWIND_WIDTH = 0.02
FRICTION = 0.002
RATE_SCALE = 0.1

F32 = jnp.float32
BF16 = jnp.bfloat16
NN = (((1,), (0,)), ((), ()))
NT = (((1,), (1,)), ((), ()))


def dot(a, b, dims=NN):
    return lax.dot_general(a, b, dims, preferred_element_type=F32)


def iota(shape, dim):
    return lax.broadcasted_iota(jnp.int32, shape, dim)


def split(x, parts):
    terms = []
    for _ in range(parts):
        head = x.astype(BF16).astype(F32)
        terms.append(head)
        x = x - head
    return terms


def mobility_of(press, dpress, water, dwater, gas, dgas):
    satur = (water, 1.0 - water - gas, gas)
    dsatur = (dwater, -dwater - dgas, dgas)
    out = []
    for a in range(3):
        volume = jnp.exp(COMPRESS[a] * (press - 1.0))
        mass = satur[a] * volume
        cdp = COMPRESS[a] * dpress
        scaled = mass * (1.0 / VISCOSITY[a])
        mob = scaled * satur[a]
        dmob = scaled * (2.0 * dsatur[a] + satur[a] * cdp)
        dmass = volume * dsatur[a] + mass * cdp
        out.append((mob, dmob, mass, dmass))
    return out


def upwind_of(pot):
    return 0.5 * jnp.tanh(pot * (0.5 / UPWIND_WIDTH)) + 0.5


def face_terms(trans, pot, dpot):
    up = upwind_of(pot)
    dup = up * (1.0 - up) * (dpot * (1.0 / UPWIND_WIDTH))
    return up, dup, trans * pot, trans * dpot


def face_flux(terms, mob_in, dmob_in, mob_out, dmob_out):
    up, dup, tpot, tdpot = terms
    diff = mob_in - mob_out
    mob = mob_out + up * diff
    dmob = dmob_out + up * (dmob_in - dmob_out) + dup * diff
    return mob * tpot, dmob * tpot + mob * tdpot


def column_to_row(eye, column):
    return jnp.sum(jnp.where(eye, column, 0.0), axis=0, keepdims=True)


def located(code, all_rows, first_row):
    if all_rows & (all_rows - 1) == 0:
        lx = code >> (all_rows.bit_length() - 1)
        row = code & (all_rows - 1)
    else:
        lx = code // all_rows
        row = code - lx * all_rows
    return lx, row - first_row


def as_column(line):
    n = line.shape[1]
    diag = iota((n, n), 0) == iota((n, n), 1)
    return jnp.sum(jnp.where(diag, line, 0.0), axis=1, keepdims=True)


def list_wells(owned, active):
    wells = owned.shape[0]
    has = jnp.max(jnp.where(owned, 1.0, 0.0), axis=1, keepdims=True)
    count = jnp.int32(0)
    for part in range(0, wells, 16):
        size = min(16, wells - part)
        bit = (1 << iota((size, 1), 0)).astype(F32)
        bits = jnp.sum(has[part : part + size] * bit).astype(jnp.int32)
        for w in range(size):
            active[1 + count] = part + w
            count = count + ((bits >> w) & 1)
    active[0] = count
    for k in range(3):
        active[1 + count + k] = wells
    return count


def outer_flux(first, last, prev, after, has_prev, has_next, layers):
    def pick(x, q):
        return x[layers * q : layers * (q + 1)]

    ins = [jnp.concatenate([pick(prev, q), pick(last, q)], axis=0) for q in range(7)]
    outs = [jnp.concatenate([pick(first, q), pick(after, q)], axis=0) for q in range(6)]
    props = [mobility_of(*(x[q] for q in (0, 3, 1, 4, 2, 5))) for x in (ins, outs)]
    terms = face_terms(ins[6], ins[0] - outs[0], ins[3] - outs[3])
    fluxes = [
        face_flux(terms, props[0][a][0], props[0][a][1], props[1][a][0], props[1][a][1])
        for a in range(3)
    ]
    before = iota((2 * layers, first.shape[1]), 0) < layers
    valid = jnp.where(before, has_prev.astype(jnp.int32), has_next.astype(jnp.int32)) == 1
    return [jnp.where(valid, f, 0.0) for t in (0, 1) for f in (x[t] for x in fluxes)]


def wells_kernel(
    all_rows,
    perf_hbm,
    press_hbm,
    satur_hbm,
    direc_hbm,
    seg_p_hbm,
    seg_d_hbm,
    wi_hbm,
    guide_hbm,
    group_hbm,
    mode_hbm,
    bhp_hbm,
    group_target_hbm,
    trans_hbm,
    send,
    rates,
    rowloc,
    lxs,
    perf,
    press,
    satur,
    direc,
    seg_p,
    seg_d,
    wi,
    guide,
    group,
    mode,
    bhp,
    group_target,
    t_col,
    held,
    held_low,
    gath,
    active,
    sems,
):
    layers, cols, rows = press.shape
    cells = layers * cols
    wells, segs = seg_p.shape
    gx, gy = lax.axis_size("gx"), lax.axis_size("gy")
    xi, yi = lax.axis_index("gx"), lax.axis_index("gy")
    share = wells // gy
    moves = [
        pltpu.make_async_copy(src, dst, sems.at[k])
        for k, (src, dst) in enumerate(
            [
                (perf_hbm, perf),
                (press_hbm, press),
                (satur_hbm, satur),
                (direc_hbm, direc),
                (seg_p_hbm, seg_p),
                (seg_d_hbm, seg_d),
                (wi_hbm, wi),
                (guide_hbm, guide),
                (group_hbm, group),
                (mode_hbm, mode),
                (bhp_hbm, bhp),
                (group_target_hbm, group_target),
                (trans_hbm.at[0, :, pl.ds(cols - 8, 8), :], t_col),
            ]
        )
    ]
    for move in moves:
        move.start()

    for move in moves:
        move.wait()

    lx_all, row_all = located(perf[...], all_rows, yi * rows)
    owned = (row_all >= 0) & (row_all < rows)
    nowhere = jnp.full((8, segs), -1, jnp.int32)
    lxs[0:wells, :] = lx_all
    rowloc[0:wells, :] = jnp.where(owned, row_all, -1)
    lxs[wells : wells + 8, :] = nowhere
    rowloc[wells : wells + 8, :] = nowhere
    count = list_wells(owned, active)

    spot = iota((wells, 128), 1) - iota((wells, 128), 0)
    guides = jnp.where(spot == 3 * wells, as_column(guide[...]), 0.0)
    groups = jnp.where(spot == 0, as_column(group[...].astype(F32)), 0.0)
    groups = jnp.sum(groups, axis=0, keepdims=True)

    pick = iota((share, wells), 1) == iota((share, wells), 0) + yi * share

    def own(line):
        return jnp.sum(jnp.where(pick, line, 0.0), axis=1, keepdims=True)

    number = own(group[...].astype(F32))
    member = number == iota((share, 128), 1).astype(F32)
    columns = [
        own(mode[...].astype(F32)),
        own(guide[...]),
        number,
        jnp.sum(jnp.where(member, group_target[...], 0.0), axis=1, keepdims=True),
        own(bhp[...]),
    ]
    lane = iota((share, 128), 1)
    info = jnp.zeros((share, 128), F32)
    for k, column in enumerate(columns):
        info = jnp.where(lane == k, column, info)
    for q in range(6):
        rates[q, wells : wells + 8, :] = jnp.zeros((8, segs), F32)
    rates[0, wells + 4 : wells + 4 + share, :] = info

    edges = [[], []]
    fields = [press, satur.at[0], satur.at[1], direc.at[0], direc.at[1], direc.at[2]]
    for q, field in enumerate(fields):
        block = field[...].reshape(cells, rows)
        terms = split(block, 3 if q == 0 else 2)
        held[q, :, 0:rows] = terms[0].astype(BF16)
        held[q, :, rows : 2 * rows] = terms[1].astype(BF16)
        if q == 0:
            held_low[...] = terms[2].astype(BF16)
        for z in range(layers):
            edges[0].append(field[z, 0:1, :])
            edges[1].append(field[z, cols - 1 : cols, :])
    for z in range(layers):
        last = t_col[z, 7:8, :]
        edges[0].append(jnp.zeros_like(last))
        edges[1].append(last)
    chunk = send.shape[1]
    for side, step in ((0, -1), (1, 1)):
        there = xi + step
        edge = jnp.concatenate(edges[side], axis=0)

        @pl.when((there >= 0) & (there < gx))
        def _(edge=edge, to=there * gy + yi):
            send[pl.ds(to, 1), 0 : 7 * layers, :] = edge[None]

    def gather_wells(at, width):
        ids = [active[1 + at + k] for k in range(width)]
        row = jnp.concatenate([rowloc[pl.ds(w, 1), :] for w in ids], axis=1)
        lx = jnp.concatenate([lxs[pl.ds(w, 1), :] for w in ids], axis=1)
        hot = jnp.where(iota((rows, width * segs), 0) == row, 1.0, 0.0).astype(BF16)
        hot2 = jnp.concatenate([hot, hot], axis=0)
        here = iota((cells, width * segs), 0) == lx
        for q in range(len(fields)):
            found = dot(held[q], hot2)
            if q == 0:
                found = found + dot(held_low[...], hot)
            line = jnp.sum(jnp.where(here, found, 0.0), axis=0, keepdims=True)
            for k, w in enumerate(ids):
                gath[q, pl.ds(w, 1), :] = line[:, k * segs : (k + 1) * segs]

    def gather_step(i, carry):
        gather_wells(4 * i, 4)
        return carry

    fours = (count + 1) // 4
    lax.fori_loop(0, fours, gather_step, 0)

    @pl.when(count > 4 * fours)
    def _():
        gather_wells(4 * fours, 2)

    vals = [gath[q, 0:wells, :] for q in range(len(fields))]
    props = mobility_of(vals[0], vals[3], vals[1], vals[4], vals[2], vals[5])
    drop = vals[0] - seg_p[...]
    ddrop = vals[3] - seg_d[...]
    weight = wi[...]
    total = jnp.zeros((wells, segs), F32)
    dtotal = jnp.zeros((wells, segs), F32)
    line = guides
    for a in range(3):
        mob, dmob = props[a][0], props[a][1]
        rate = jnp.where(owned, weight * mob * drop, 0.0)
        drate = jnp.where(owned, weight * (dmob * drop + mob * ddrop), 0.0)
        total = total + rate
        dtotal = dtotal + drate
        rates[a, 0:wells, :] = rate
        rates[3 + a, 0:wells, :] = drate
        of_well = jnp.sum(rate, axis=1, keepdims=True)
        line = jnp.where(spot == a * wells, of_well, line)
    line = jnp.sum(line, axis=0, keepdims=True)
    lines = jnp.concatenate([line, groups], axis=0)
    for y in range(gy):
        both = jnp.concatenate(
            [total[y * share : (y + 1) * share], dtotal[y * share : (y + 1) * share]], axis=0
        )
        send[pl.ds(xi * gy + y, 1), 0 : 2 * share, :] = both[None]
    for to in range(gx * gy):
        send[to, chunk - 2 : chunk, :] = lines


def cells_kernel(
    press,
    satur,
    pore,
    trans,
    direc,
    parent,
    seg_p,
    seg_d,
    head,
    inner,
    reach,
    known,
    edges,
    inside_pair,
    between_pairs,
    mobs,
    base,
):
    layers, cols, rows = press.shape
    chunks = cols // 8
    wells, segs = seg_p.shape
    share = reach.shape[0]
    start = lax.axis_index("gy") * share

    eye = iota((cols, rows), 0) == iota((cols, rows), 1)
    fields = [press, satur.at[0], satur.at[1], direc.at[0], direc.at[1], direc.at[2]]
    for side in range(4):
        lines = fields + [trans.at[side // 2]]
        for q, field in enumerate(lines):
            for z in range(layers):
                if q == 6 and side % 2 == 0:
                    line = jnp.zeros((1, rows), F32)
                elif side < 2:
                    line = field[z, 0:1, :] if side == 0 else field[z, cols - 1 : cols, :]
                else:
                    at = 0 if side == 2 else rows - 1
                    line = column_to_row(eye, field[z, :, at : at + 1])
                edges[side, q * layers + z : q * layers + z + 1, :] = line
    even = lax.rem(lax.axis_index("gy"), 2) == 0
    inside_pair[...] = jnp.where(even, edges[3], edges[2])
    between_pairs[...] = jnp.where(even, edges[2], edges[3])

    sub, lane = iota((segs, segs), 0), iota((segs, segs), 1)
    pad = jnp.zeros((10, segs), F32)
    mine = pl.ds(start, share)
    p_own, d_own = seg_p[mine, :], seg_d[mine, :]
    reaches, aboves, daboves = [], [], []
    for i in range(share):
        link = sub == parent[pl.ds(start + i, 1), :]
        reaches.append(jnp.where(link | (sub == lane), 1.0, 0.0).astype(BF16))
        lines = split(p_own[i : i + 1], 3) + split(d_own[i : i + 1], 3) + [pad]
        lines = jnp.concatenate(lines, axis=0).astype(BF16)
        found = dot(lines, jnp.where(link, 1.0, 0.0).astype(BF16))
        aboves.append(found[0:1] + found[1:2] + found[2:3])
        daboves.append(found[3:4] + found[4:5] + found[5:6])
    above, dabove = jnp.concatenate(aboves, axis=0), jnp.concatenate(daboves, axis=0)
    first = iota((share, segs), 1) == 0
    known[0:share, :] = jnp.where(first, p_own, p_own - above - head[mine, :])
    known[share : 2 * share, :] = jnp.where(first, d_own, d_own - dabove)

    for c in range(chunks):
        at = slice(8 * c, 8 * c + 8)
        for z in range(layers):
            p, dp = press[z, at, :], direc[0, z, at, :]
            props = mobility_of(
                p, dp, satur[0, z, at, :], direc[1, z, at, :], satur[1, z, at, :], direc[2, z, at, :]
            )
            rock = 1.0 + ROCK_COMP * (p - 1.0)
            drock = ROCK_COMP * dp
            pv = pore[z, at, :]
            for a in range(3):
                mob, dmob, mass, dmass = props[a]
                mobs[a, z, at, :] = mob
                mobs[3 + a, z, at, :] = dmob
                base[a, z, at, :] = pv * (rock * mass)
                base[3 + a, z, at, :] = pv * (drock * mass + rock * dmass)

    sub = iota((8, rows), 0)
    lane = iota((8, rows), 1)
    levels = (segs - 1).bit_length()
    refs = [press, direc.at[0]] + [mobs.at[k] for k in range(6)]

    def load(c):
        held = [[ref[z, 8 * c : 8 * c + 8, :] for ref in refs] for z in range(layers)]
        return held, [[pltpu.roll(x, 7, 0) for x in line] for line in held]

    before = [[jnp.zeros((8, rows), F32)] * layers for _ in range(6)]
    now, up = load(0)
    for c in range(chunks):
        at = slice(8 * c, 8 * c + 8)
        last_chunk = c == chunks - 1
        if not last_chunk:
            later, up_later = load(c + 1)
        sums = []
        for z in range(layers):
            if last_chunk:
                nexts = up[z]
            else:
                nexts = [jnp.where(sub == 7, x, y) for x, y in zip(up_later[z], up[z])]
            sides = [pltpu.roll(x, rows - 1, 1) for x in now[z]]
            p, dp = now[z][0:2]
            t_col, t_row = trans[0, z, at, :], trans[1, z, at, :]
            if last_chunk:
                t_col = jnp.where(sub == 7, 0.0, t_col)
            t_row = jnp.where(lane == rows - 1, 0.0, t_row)
            col = face_terms(t_col, p - nexts[0], dp - nexts[1])
            row = face_terms(t_row, p - sides[0], dp - sides[1])
            divergence = []
            for a in range(3):
                m, dm = now[z][2 + a], now[z][5 + a]
                flux_col = face_flux(col, m, dm, nexts[2 + a], nexts[5 + a])
                flux_row = face_flux(row, m, dm, sides[2 + a], sides[5 + a])
                both = []
                for t in (0, 1):
                    f, g = flux_col[t], flux_row[t]
                    rolled = pltpu.roll(f, 1, 0)
                    down = jnp.where(sub == 0, before[3 * t + a][z], rolled)
                    before[3 * t + a][z] = rolled
                    both.append(base[3 * t + a, z, at, :] + (f - down) + (g - pltpu.roll(g, 1, 1)))
                divergence.append(both)
            sums.append(divergence)
        for z in range(layers - 1):
            dpot = now[z][1] - now[z + 1][1]
            t_lay = trans[2, z, at, :]
            for a in range(3):
                pot = now[z][0] - now[z + 1][0] + DENSITY[a] * GRAVITY
                terms = face_terms(t_lay, pot, dpot)
                flux = face_flux(
                    terms, now[z][2 + a], now[z][5 + a], now[z + 1][2 + a], now[z + 1][5 + a]
                )
                for t in (0, 1):
                    sums[z][a][t] = sums[z][a][t] + flux[t]
                    sums[z + 1][a][t] = sums[z + 1][a][t] - flux[t]
        for z in range(layers):
            for a in range(3):
                for t in (0, 1):
                    inner[3 * t + a, z, at, :] = sums[z][a][t]
        if not last_chunk:
            now, up = later, up_later
        if c % 2 == 1 and c // 2 < levels:
            for i in range(share):
                reaches[i] = jnp.minimum(dot(reaches[i], reaches[i]), 1.0).astype(BF16)
    for level in range(chunks // 2, levels):
        for i in range(share):
            reaches[i] = jnp.minimum(dot(reaches[i], reaches[i]), 1.0).astype(BF16)
    for i in range(share):
        reach[i] = reaches[i]


def scatter_kernel(
    inner,
    old_mass,
    rates,
    rowloc,
    lxs,
    acc,
    packed,
    active,
):
    layers, cols, rows = acc.shape[1:]
    cells = layers * cols
    wells, segs = rates.shape[1] - 8, rates.shape[2]
    count = list_wells(rowloc[0:wells, :] >= 0, active)
    packed[...] = rates[0, wells + 4 : wells + 4 + packed.shape[0], :]

    for k in range(6):
        acc[k] = inner[k] - old_mass[k] if k < 3 else inner[k]

    sub_row = iota((rows, 4 * segs), 0)
    sub_lx = iota((cells, 4 * segs), 0)

    def scatter_wells(i, carry):
        ids = [active[1 + 4 * i + k] for k in range(4)]
        row = jnp.concatenate([rowloc[pl.ds(w, 1), :] for w in ids], axis=1)
        lx = jnp.concatenate([lxs[pl.ds(w, 1), :] for w in ids], axis=1)
        at = sub_row == row
        hot = jnp.where(sub_lx == lx, 1.0, 0.0).astype(BF16)
        hot = jnp.concatenate([hot, hot], axis=1)
        for q in range(0, 6, 2):
            both = []
            for k in (q, q + 1):
                rate = jnp.concatenate([rates[k, pl.ds(w, 1), :] for w in ids], axis=1)
                terms = [jnp.where(at, term, 0.0).astype(BF16) for term in split(rate, 2)]
                both.append(jnp.concatenate(terms, axis=1))
            part = dot(hot, jnp.concatenate(both, axis=0), NT)
            acc[q] = acc[q] + part[:, 0:rows].reshape(layers, cols, rows)
            acc[q + 1] = acc[q + 1] + part[:, rows : 2 * rows].reshape(layers, cols, rows)
        return carry

    lax.fori_loop(0, (count + 3) // 4, scatter_wells, 0)


def sides_kernel(
    acc, edges, inside_pair, between_pairs, out_hbm, dout_hbm, rims, out, turned, sems
):
    layers, cols, rows = out.shape[1:]
    gy, yi = lax.axis_size("gy"), lax.axis_index("gy")
    even = lax.rem(yi, 2) == 0
    one, other = inside_pair[...], between_pairs[...]
    prev, after = jnp.where(even, other, one), jnp.where(even, one, other)
    flux = outer_flux(edges[2], edges[3], prev, after, yi > 0, yi < gy - 1, layers)
    spare = jnp.zeros((128 - 12 * layers, rows), F32)
    turned[...] = jnp.concatenate(flux + [spare], axis=0).T
    lane = iota((cols, rows), 1)
    moves = []
    for k in range(6):
        for z in range(layers):
            j = 2 * layers * k + z
            before = turned[:, j : j + 1]
            behind = turned[:, j + layers : j + layers + 1]
            side = jnp.where(lane == 0, -before, jnp.where(lane == rows - 1, behind, 0.0))
            out[k, z] = acc[k, z] + side
            rims[k, 0, z] = out[k, z, 0:8, :]
            rims[k, 1, z] = out[k, z, cols - 8 : cols, :]
        final = out_hbm.at[k] if k < 3 else dout_hbm.at[k - 3]
        moves.append(pltpu.make_async_copy(out.at[k], final, sems.at[k]))
        moves[k].start()
    for move in moves:
        move.wait()


def finish_kernel(
    wells,
    out_before,
    dout_before,
    rims,
    reach,
    known,
    packed,
    edges,
    got,
    out_hbm,
    dout_hbm,
    seg_out_hbm,
    seg_dout_hbm,
    group_out_hbm,
    tiles,
    seg_out,
    seg_dout,
    group_out,
    sems,
):
    del out_before, dout_before
    layers = tiles.shape[3]
    cols = out_hbm.shape[2]
    share, segs = seg_out.shape
    gx, gy = lax.axis_size("gx"), lax.axis_size("gy")
    xi, yi = lax.axis_index("gx"), lax.axis_index("gy")
    chunk = got.shape[1]

    has_prev, has_next = xi > 0, xi < gx - 1
    prev, after = (
        got[pl.ds(jnp.where(inside, x * gy + yi, 0), 1), 0 : 7 * layers, :][0]
        for inside, x in ((has_prev, xi - 1), (has_next, xi + 1))
    )
    flux = outer_flux(edges[0], edges[1], prev, after, has_prev, has_next, layers)
    moves = []

    def write(src, dst):
        move = pltpu.make_async_copy(src, dst, sems.at[len(moves)])
        move.start()
        moves.append(move)

    for t, final in ((0, out_hbm), (1, dout_hbm)):
        for side, at in ((0, 0), (1, 7)):
            for a in range(3):
                k = 3 * t + a
                for z in range(layers):
                    tiles[t, side, a, z] = rims[k, side, z]
                    f = flux[k][side * layers + z : side * layers + z + 1]
                    line = rims[k, side, z, at : at + 1, :]
                    tiles[t, side, a, z, at : at + 1, :] = line - f if side == 0 else line + f
            write(tiles.at[t, side], final.at[:, :, pl.ds(side * (cols - 8), 8), :])

    total = got[xi * gy, 0 : 2 * share, :]
    for y in range(1, gy):
        total = total + got[xi * gy + y, 0 : 2 * share, :]

    lines, numbers = [], []
    for x in range(gx):
        line = got[x * gy, chunk - 2 : chunk - 1, :]
        more = line
        for y in range(1, gy):
            more = more + got[x * gy + y, chunk - 2 : chunk - 1, :]
        lines.append(jnp.where(iota((1, 128), 1) < 3 * wells, more, line))
        numbers.append(got[x * gy, chunk - 1 : chunk, :])
    columns = jnp.concatenate(lines + numbers + [jnp.zeros((128 - 2 * gx, 128), F32)], axis=0).T
    group_sums = [jnp.zeros((wells, 128), F32)] * 4
    for x in range(gx):
        member = columns[0:wells, gx + x : gx + x + 1] == iota((wells, 128), 1).astype(F32)
        for a in range(4):
            values = columns[a * wells : (a + 1) * wells, x : x + 1]
            group_sums[a] = group_sums[a] + jnp.where(member, values, 0.0)
    for a in range(3):
        group_out[a : a + 1, :] = jnp.sum(group_sums[a], axis=0, keepdims=True)
    write(group_out, group_out_hbm)
    guide_total = jnp.sum(group_sums[3], axis=0, keepdims=True)

    flows, dflows = [], []
    pad = jnp.zeros((10, segs), F32)
    for i in range(share):
        lines = split(total[i : i + 1], 3) + split(total[share + i : share + i + 1], 3) + [pad]
        flow = dot(jnp.concatenate(lines, axis=0).astype(BF16), reach[i], NT)
        flows.append(flow[0:1] + flow[1:2] + flow[2:3])
        dflows.append(flow[3:4] + flow[4:5] + flow[5:6])
    flow, dflow = jnp.concatenate(flows, axis=0), jnp.concatenate(dflows, axis=0)
    column = [packed[:, k : k + 1] for k in range(5)]
    member = column[2] == iota((share, 128), 1).astype(F32)
    of_group = jnp.sum(jnp.where(member, guide_total, 0.0), axis=1, keepdims=True)
    target = column[3] * column[1] / of_group
    by_rate = column[0] == 1.0
    first = iota((share, segs), 1) == 0
    limit, dlimit = known[0:share, :], known[share : 2 * share, :]
    root = jnp.where(by_rate, RATE_SCALE * (flow - target), limit - column[4])
    droot = jnp.where(by_rate, RATE_SCALE * dflow, dlimit)
    seg_out[...] = jnp.where(first, root, limit - FRICTION * flow)
    seg_dout[...] = jnp.where(first, droot, dlimit - FRICTION * dflow)
    write(seg_out, seg_out_hbm)
    write(seg_dout, seg_dout_hbm)
    for move in moves:
        move.wait()


VMEM = pl.BlockSpec(memory_space=pltpu.VMEM)
ANY = pl.BlockSpec(memory_space=pl.ANY)


def params(mebibytes):
    return pltpu.CompilerParams(vmem_limit_bytes=mebibytes * 1024 * 1024)


def per_device(
    pressure,
    saturations,
    old_mass,
    pore_volume,
    transmissibility,
    direction,
    seg_pressure,
    seg_direction,
    perf_cell,
    well_index,
    parent,
    seg_head,
    well_mode,
    bhp_limit,
    guide_rate,
    group_of,
    group_target,
):
    layers, cols, rows = pressure.shape
    wells, segs = seg_pressure.shape
    cells = layers * cols
    gx, gy = lax.axis_size("gx"), lax.axis_size("gy")
    share = wells // gy
    edge_rows = 7 * layers
    chunk = 2 + max(2 * share, edge_rows)
    shape = jax.ShapeDtypeStruct

    guide_line = guide_rate.reshape(1, wells)
    group_line = group_of.reshape(1, wells)
    send, rates, rowloc, lxs = pl.pallas_call(
        functools.partial(wells_kernel, rows * gy),
        out_shape=(
            shape((gx * gy, chunk, 128), F32),
            shape((6, wells + 8, segs), F32),
            shape((wells + 8, segs), jnp.int32),
            shape((wells + 8, segs), jnp.int32),
        ),
        in_specs=[ANY] * 13,
        out_specs=(VMEM,) * 4,
        scratch_shapes=[
            pltpu.VMEM((wells, segs), jnp.int32),
            pltpu.VMEM((layers, cols, rows), F32),
            pltpu.VMEM((2, layers, cols, rows), F32),
            pltpu.VMEM((3, layers, cols, rows), F32),
            pltpu.VMEM((wells, segs), F32),
            pltpu.VMEM((wells, segs), F32),
            pltpu.VMEM((wells, segs), F32),
            pltpu.VMEM((1, wells), F32),
            pltpu.VMEM((1, wells), jnp.int32),
            pltpu.VMEM((1, wells), jnp.int32),
            pltpu.VMEM((1, wells), F32),
            pltpu.VMEM((1, 128), F32),
            pltpu.VMEM((layers, 8, rows), F32),
            pltpu.VMEM((6, cells, 2 * rows), BF16),
            pltpu.VMEM((cells, rows), BF16),
            pltpu.VMEM((6, wells + 8, segs), F32),
            pltpu.SMEM((wells + 8,), jnp.int32),
            pltpu.SemaphoreType.DMA((13,)),
        ],
        compiler_params=params(56),
        name="wells",
    )(
        perf_cell,
        pressure,
        saturations,
        direction,
        seg_pressure,
        seg_direction,
        well_index,
        guide_line,
        group_line,
        well_mode.reshape(1, wells),
        bhp_limit.reshape(1, wells),
        group_target.reshape(1, 128),
        transmissibility,
    )

    got = lax.all_to_all(send, ("gx", "gy"), 0, 0, tiled=True)

    seg_head, rowloc = lax.optimization_barrier((seg_head, rowloc))

    inner, reach, known, edges, inside_pair, between_pairs = pl.pallas_call(
        cells_kernel,
        out_shape=(
            shape((6, layers, cols, rows), F32),
            shape((share, segs, segs), BF16),
            shape((2 * share, segs), F32),
            shape((4, edge_rows, 128), F32),
            shape((edge_rows, 128), F32),
            shape((edge_rows, 128), F32),
        ),
        in_specs=[VMEM] * 9,
        out_specs=(VMEM,) * 6,
        scratch_shapes=[
            pltpu.VMEM((6, layers, cols, rows), F32),
            pltpu.VMEM((6, layers, cols, rows), F32),
        ],
        compiler_params=params(32),
        cost_estimate=pl.CostEstimate(flops=300_000_000, bytes_accessed=4_000_000, transcendentals=400_000),
        name="cells",
    )(
        pressure,
        saturations,
        pore_volume,
        transmissibility,
        direction,
        parent,
        seg_pressure,
        seg_direction,
        seg_head,
    )

    def swap(x, first):
        pairs = [(i, i + 1) for i in range(first, gy - 1, 2)]
        return lax.ppermute(x, "gy", pairs + [(j, i) for i, j in pairs])

    inside_pair = swap(inside_pair, 0)
    between_pairs = swap(between_pairs, 1)

    cell_shape = shape((3, layers, cols, rows), F32)
    summed, packed = pl.pallas_call(
        scatter_kernel,
        out_shape=(shape((6, layers, cols, rows), F32), shape((share, 128), F32)),
        in_specs=[VMEM] * 5,
        out_specs=(VMEM, VMEM),
        scratch_shapes=[pltpu.SMEM((wells + 8,), jnp.int32)],
        compiler_params=params(32),
        cost_estimate=pl.CostEstimate(flops=300_000_000, bytes_accessed=4_000_000, transcendentals=0),
        name="scatter",
    )(
        inner,
        old_mass,
        rates,
        rowloc,
        lxs,
    )

    out, dout, rims = pl.pallas_call(
        sides_kernel,
        out_shape=(cell_shape, cell_shape, shape((6, 2, layers, 8, rows), F32)),
        in_specs=[VMEM] * 4,
        out_specs=(ANY, ANY, VMEM),
        scratch_shapes=[
            pltpu.VMEM((6, layers, cols, rows), F32),
            pltpu.VMEM((cols, 128), F32),
            pltpu.SemaphoreType.DMA((6,)),
        ],
        compiler_params=params(32),
        cost_estimate=pl.CostEstimate(flops=3_000_000, bytes_accessed=4_000_000, transcendentals=10_000),
        name="sides",
    )(summed, edges, inside_pair, between_pairs)

    out, dout, seg_out, seg_dout, groups = pl.pallas_call(
        functools.partial(finish_kernel, wells),
        out_shape=(
            cell_shape,
            cell_shape,
            shape((share, segs), F32),
            shape((share, segs), F32),
            shape((3, 128), F32),
        ),
        in_specs=[ANY] * 2 + [VMEM] * 6,
        out_specs=(ANY,) * 5,
        input_output_aliases={0: 0, 1: 1},
        scratch_shapes=[
            pltpu.VMEM((2, 2, 3, layers, 8, rows), F32),
            pltpu.VMEM((share, segs), F32),
            pltpu.VMEM((share, segs), F32),
            pltpu.VMEM((3, 128), F32),
            pltpu.SemaphoreType.DMA((7,)),
        ],
        compiler_params=params(32),
        name="finish",
    )(out, dout, rims, reach, known, packed, edges, got)
    return out, dout, seg_out, seg_dout, groups


def solution(mesh):
    placed = (
        P(None, "gx", "gy"),
        P(None, None, "gx", "gy"),
        P(None, None, "gx", "gy"),
        P(None, "gx", "gy"),
        P(None, None, "gx", "gy"),
        P(None, None, "gx", "gy"),
        P("gx", None),
        P("gx", None),
        P("gx", None),
        P("gx", None),
        P("gx", None),
        P("gx", None),
        P("gx"),
        P("gx"),
        P("gx"),
        P("gx", None),
        P(),
    )
    return jax.shard_map(
        per_device,
        mesh=mesh,
        in_specs=placed,
        out_specs=(
            P(None, None, "gx", "gy"),
            P(None, None, "gx", "gy"),
            P(("gx", "gy"), None),
            P(("gx", "gy"), None),
            P(),
        ),
        check_vma=False,
    )
```

```python
import functools

import jax
import jax.numpy as jnp
from jax import lax
from jax.experimental import pallas as pl
from jax.experimental.pallas import tpu as pltpu
from jax.sharding import PartitionSpec as P

COMPRESS = (0.05, 0.2, 1.0)
VISCOSITY = (0.5, 1.0, 0.2)
DENSITY = (1.0, 0.8, 0.2)
ROCK_COMP = 0.01
GRAVITY = 0.05
UPWIND_WIDTH = 0.02
FRICTION = 0.002
RATE_SCALE = 0.1

F32 = jnp.float32
BF16 = jnp.bfloat16
NN = (((1,), (0,)), ((), ()))
NT = (((1,), (1,)), ((), ()))


def dot(a, b, dims=NN):
    return lax.dot_general(a, b, dims, preferred_element_type=F32)


def iota(shape, dim):
    return lax.broadcasted_iota(jnp.int32, shape, dim)


def split(x, parts):
    terms = []
    for _ in range(parts):
        head = x.astype(BF16).astype(F32)
        terms.append(head)
        x = x - head
    return terms


def mobility_of(press, dpress, water, dwater, gas, dgas):
    satur = (water, 1.0 - water - gas, gas)
    dsatur = (dwater, -dwater - dgas, dgas)
    out = []
    for a in range(3):
        volume = jnp.exp(COMPRESS[a] * (press - 1.0))
        mass = satur[a] * volume
        cdp = COMPRESS[a] * dpress
        scaled = mass * (1.0 / VISCOSITY[a])
        mob = scaled * satur[a]
        dmob = scaled * (2.0 * dsatur[a] + satur[a] * cdp)
        dmass = volume * dsatur[a] + mass * cdp
        out.append((mob, dmob, mass, dmass))
    return out


def upwind_of(pot):
    return 0.5 * jnp.tanh(pot * (0.5 / UPWIND_WIDTH)) + 0.5


def face_terms(trans, pot, dpot):
    up = upwind_of(pot)
    dup = up * (1.0 - up) * (dpot * (1.0 / UPWIND_WIDTH))
    return up, dup, trans * pot, trans * dpot


def face_flux(terms, mob_in, dmob_in, mob_out, dmob_out):
    up, dup, tpot, tdpot = terms
    diff = mob_in - mob_out
    mob = mob_out + up * diff
    dmob = dmob_out + up * (dmob_in - dmob_out) + dup * diff
    return mob * tpot, dmob * tpot + mob * tdpot


def column_to_row(eye, column):
    return jnp.sum(jnp.where(eye, column, 0.0), axis=0, keepdims=True)


def located(code, all_rows, first_row):
    if all_rows & (all_rows - 1) == 0:
        lx = code >> (all_rows.bit_length() - 1)
        row = code & (all_rows - 1)
    else:
        lx = code // all_rows
        row = code - lx * all_rows
    return lx, row - first_row


def as_column(line):
    n = line.shape[1]
    diag = iota((n, n), 0) == iota((n, n), 1)
    return jnp.sum(jnp.where(diag, line, 0.0), axis=1, keepdims=True)


def list_wells(owned, active):
    wells = owned.shape[0]
    has = jnp.max(jnp.where(owned, 1.0, 0.0), axis=1, keepdims=True)
    count = jnp.int32(0)
    for part in range(0, wells, 16):
        size = min(16, wells - part)
        bit = (1 << iota((size, 1), 0)).astype(F32)
        bits = jnp.sum(has[part : part + size] * bit).astype(jnp.int32)
        for w in range(size):
            active[1 + count] = part + w
            count = count + ((bits >> w) & 1)
    active[0] = count
    for k in range(3):
        active[1 + count + k] = wells
    return count


def outer_flux(first, last, prev, after, has_prev, has_next, layers):
    def pick(x, q):
        return x[layers * q : layers * (q + 1)]

    ins = [jnp.concatenate([pick(prev, q), pick(last, q)], axis=0) for q in range(7)]
    outs = [jnp.concatenate([pick(first, q), pick(after, q)], axis=0) for q in range(6)]
    props = [mobility_of(*(x[q] for q in (0, 3, 1, 4, 2, 5))) for x in (ins, outs)]
    terms = face_terms(ins[6], ins[0] - outs[0], ins[3] - outs[3])
    fluxes = [
        face_flux(terms, props[0][a][0], props[0][a][1], props[1][a][0], props[1][a][1])
        for a in range(3)
    ]
    before = iota((2 * layers, first.shape[1]), 0) < layers
    valid = jnp.where(before, has_prev.astype(jnp.int32), has_next.astype(jnp.int32)) == 1
    return [jnp.where(valid, f, 0.0) for t in (0, 1) for f in (x[t] for x in fluxes)]


def wells_kernel(
    all_rows,
    perf_hbm,
    press_hbm,
    satur_hbm,
    direc_hbm,
    seg_p_hbm,
    seg_d_hbm,
    wi_hbm,
    guide_hbm,
    group_hbm,
    mode_hbm,
    bhp_hbm,
    group_target_hbm,
    trans_hbm,
    send,
    rates,
    rowloc,
    lxs,
    perf,
    press,
    satur,
    direc,
    seg_p,
    seg_d,
    wi,
    guide,
    group,
    mode,
    bhp,
    group_target,
    t_col,
    held,
    held_low,
    gath,
    active,
    sems,
):
    layers, cols, rows = press.shape
    cells = layers * cols
    wells, segs = seg_p.shape
    gx, gy = lax.axis_size("gx"), lax.axis_size("gy")
    xi, yi = lax.axis_index("gx"), lax.axis_index("gy")
    share = wells // gy
    moves = [
        pltpu.make_async_copy(src, dst, sems.at[k])
        for k, (src, dst) in enumerate(
            [
                (perf_hbm, perf),
                (press_hbm, press),
                (satur_hbm, satur),
                (direc_hbm, direc),
                (seg_p_hbm, seg_p),
                (seg_d_hbm, seg_d),
                (wi_hbm, wi),
                (guide_hbm, guide),
                (group_hbm, group),
                (mode_hbm, mode),
                (bhp_hbm, bhp),
                (group_target_hbm, group_target),
                (trans_hbm.at[0, :, pl.ds(cols - 8, 8), :], t_col),
            ]
        )
    ]
    for move in moves:
        move.start()

    moves[0].wait()
    lx_all, row_all = located(perf[...], all_rows, yi * rows)
    owned = (row_all >= 0) & (row_all < rows)
    nowhere = jnp.full((8, segs), -1, jnp.int32)
    lxs[0:wells, :] = lx_all
    rowloc[0:wells, :] = jnp.where(owned, row_all, -1)
    lxs[wells : wells + 8, :] = nowhere
    rowloc[wells : wells + 8, :] = nowhere
    count = list_wells(owned, active)

    for move in moves[4:]:
        move.wait()
    spot = iota((wells, 128), 1) - iota((wells, 128), 0)
    guides = jnp.where(spot == 3 * wells, as_column(guide[...]), 0.0)
    groups = jnp.where(spot == 0, as_column(group[...].astype(F32)), 0.0)
    groups = jnp.sum(groups, axis=0, keepdims=True)

    pick = iota((share, wells), 1) == iota((share, wells), 0) + yi * share

    def own(line):
        return jnp.sum(jnp.where(pick, line, 0.0), axis=1, keepdims=True)

    number = own(group[...].astype(F32))
    member = number == iota((share, 128), 1).astype(F32)
    columns = [
        own(mode[...].astype(F32)),
        own(guide[...]),
        number,
        jnp.sum(jnp.where(member, group_target[...], 0.0), axis=1, keepdims=True),
        own(bhp[...]),
    ]
    lane = iota((share, 128), 1)
    info = jnp.zeros((share, 128), F32)
    for k, column in enumerate(columns):
        info = jnp.where(lane == k, column, info)
    for q in range(6):
        rates[q, wells : wells + 8, :] = jnp.zeros((8, segs), F32)
    rates[0, wells + 4 : wells + 4 + share, :] = info

    edges = [[], []]
    fields = [press, satur.at[0], satur.at[1], direc.at[0], direc.at[1], direc.at[2]]
    arrive = {0: 1, 1: 2, 3: 3}
    for q, field in enumerate(fields):
        if q in arrive:
            moves[arrive[q]].wait()
        block = field[...].reshape(cells, rows)
        terms = split(block, 3 if q == 0 else 2)
        held[q, :, 0:rows] = terms[0].astype(BF16)
        held[q, :, rows : 2 * rows] = terms[1].astype(BF16)
        if q == 0:
            held_low[...] = terms[2].astype(BF16)
        for z in range(layers):
            edges[0].append(field[z, 0:1, :])
            edges[1].append(field[z, cols - 1 : cols, :])
    for z in range(layers):
        last = t_col[z, 7:8, :]
        edges[0].append(jnp.zeros_like(last))
        edges[1].append(last)
    chunk = send.shape[1]
    for side, step in ((0, -1), (1, 1)):
        there = xi + step
        edge = jnp.concatenate(edges[side], axis=0)

        @pl.when((there >= 0) & (there < gx))
        def _(edge=edge, to=yi * gx + there):
            send[pl.ds(to, 1), 0 : 7 * layers, :] = edge[None]

    def gather_wells(at, width):
        ids = [active[1 + at + k] for k in range(width)]
        row = jnp.concatenate([rowloc[pl.ds(w, 1), :] for w in ids], axis=1)
        lx = jnp.concatenate([lxs[pl.ds(w, 1), :] for w in ids], axis=1)
        hot = jnp.where(iota((rows, width * segs), 0) == row, 1.0, 0.0).astype(BF16)
        hot2 = jnp.concatenate([hot, hot], axis=0)
        here = iota((cells, width * segs), 0) == lx
        for q in range(len(fields)):
            found = dot(held[q], hot2)
            if q == 0:
                found = found + dot(held_low[...], hot)
            line = jnp.sum(jnp.where(here, found, 0.0), axis=0, keepdims=True)
            for k, w in enumerate(ids):
                gath[q, pl.ds(w, 1), :] = line[:, k * segs : (k + 1) * segs]

    def gather_step(i, carry):
        gather_wells(4 * i, 4)
        return carry

    fours = (count + 1) // 4
    lax.fori_loop(0, fours, gather_step, 0)

    @pl.when(count > 4 * fours)
    def _():
        gather_wells(4 * fours, 2)

    vals = [gath[q, 0:wells, :] for q in range(len(fields))]
    props = mobility_of(vals[0], vals[3], vals[1], vals[4], vals[2], vals[5])
    drop = vals[0] - seg_p[...]
    ddrop = vals[3] - seg_d[...]
    weight = wi[...]
    total = jnp.zeros((wells, segs), F32)
    dtotal = jnp.zeros((wells, segs), F32)
    line = guides
    for a in range(3):
        mob, dmob = props[a][0], props[a][1]
        rate = jnp.where(owned, weight * mob * drop, 0.0)
        drate = jnp.where(owned, weight * (dmob * drop + mob * ddrop), 0.0)
        total = total + rate
        dtotal = dtotal + drate
        rates[a, 0:wells, :] = rate
        rates[3 + a, 0:wells, :] = drate
        of_well = jnp.sum(rate, axis=1, keepdims=True)
        line = jnp.where(spot == a * wells, of_well, line)
    line = jnp.sum(line, axis=0, keepdims=True)
    lines = jnp.concatenate([line, groups], axis=0)
    for y in range(gy):
        both = jnp.concatenate(
            [total[y * share : (y + 1) * share], dtotal[y * share : (y + 1) * share]], axis=0
        )
        send[pl.ds(y * gx + xi, 1), 0 : 2 * share, :] = both[None]
    for to in range(gx * gy):
        send[to, chunk - 2 : chunk, :] = lines


def cells_kernel(
    press,
    satur,
    pore,
    trans,
    direc,
    parent,
    seg_p,
    seg_d,
    head,
    inner,
    reach,
    known,
    edges,
    inside_pair,
    between_pairs,
    mobs,
    base,
):
    layers, cols, rows = press.shape
    chunks = cols // 8
    wells, segs = seg_p.shape
    share = reach.shape[0]
    start = lax.axis_index("gy") * share

    eye = iota((cols, rows), 0) == iota((cols, rows), 1)
    fields = [press, satur.at[0], satur.at[1], direc.at[0], direc.at[1], direc.at[2]]
    for side in range(4):
        lines = fields + [trans.at[side // 2]]
        for q, field in enumerate(lines):
            for z in range(layers):
                if q == 6 and side % 2 == 0:
                    line = jnp.zeros((1, rows), F32)
                elif side < 2:
                    line = field[z, 0:1, :] if side == 0 else field[z, cols - 1 : cols, :]
                else:
                    at = 0 if side == 2 else rows - 1
                    line = column_to_row(eye, field[z, :, at : at + 1])
                edges[side, q * layers + z : q * layers + z + 1, :] = line
    even = lax.rem(lax.axis_index("gy"), 2) == 0
    inside_pair[...] = jnp.where(even, edges[3], edges[2])
    between_pairs[...] = jnp.where(even, edges[2], edges[3])

    sub, lane = iota((segs, segs), 0), iota((segs, segs), 1)
    pad = jnp.zeros((10, segs), F32)
    mine = pl.ds(start, share)
    p_own, d_own = seg_p[mine, :], seg_d[mine, :]
    reaches, aboves, daboves = [], [], []
    for i in range(share):
        link = sub == parent[pl.ds(start + i, 1), :]
        reaches.append(jnp.where(link | (sub == lane), 1.0, 0.0).astype(BF16))
        lines = split(p_own[i : i + 1], 3) + split(d_own[i : i + 1], 3) + [pad]
        lines = jnp.concatenate(lines, axis=0).astype(BF16)
        found = dot(lines, jnp.where(link, 1.0, 0.0).astype(BF16))
        aboves.append(found[0:1] + found[1:2] + found[2:3])
        daboves.append(found[3:4] + found[4:5] + found[5:6])
    above, dabove = jnp.concatenate(aboves, axis=0), jnp.concatenate(daboves, axis=0)
    first = iota((share, segs), 1) == 0
    known[0:share, :] = jnp.where(first, p_own, p_own - above - head[mine, :])
    known[share : 2 * share, :] = jnp.where(first, d_own, d_own - dabove)

    for c in range(chunks):
        at = slice(8 * c, 8 * c + 8)
        for z in range(layers):
            p, dp = press[z, at, :], direc[0, z, at, :]
            props = mobility_of(
                p, dp, satur[0, z, at, :], direc[1, z, at, :], satur[1, z, at, :], direc[2, z, at, :]
            )
            rock = 1.0 + ROCK_COMP * (p - 1.0)
            drock = ROCK_COMP * dp
            pv = pore[z, at, :]
            for a in range(3):
                mob, dmob, mass, dmass = props[a]
                mobs[a, z, at, :] = mob
                mobs[3 + a, z, at, :] = dmob
                base[a, z, at, :] = pv * (rock * mass)
                base[3 + a, z, at, :] = pv * (drock * mass + rock * dmass)

    sub = iota((8, rows), 0)
    lane = iota((8, rows), 1)
    levels = (segs - 1).bit_length()
    refs = [press, direc.at[0]] + [mobs.at[k] for k in range(6)]

    def load(c):
        held = [[ref[z, 8 * c : 8 * c + 8, :] for ref in refs] for z in range(layers)]
        return held, [[pltpu.roll(x, 7, 0) for x in line] for line in held]

    before = [[jnp.zeros((8, rows), F32)] * layers for _ in range(6)]
    now, up = load(0)
    for c in range(chunks):
        at = slice(8 * c, 8 * c + 8)
        last_chunk = c == chunks - 1
        if not last_chunk:
            later, up_later = load(c + 1)
        sums = []
        for z in range(layers):
            if last_chunk:
                nexts = up[z]
            else:
                nexts = [jnp.where(sub == 7, x, y) for x, y in zip(up_later[z], up[z])]
            sides = [pltpu.roll(x, rows - 1, 1) for x in now[z]]
            p, dp = now[z][0:2]
            t_col, t_row = trans[0, z, at, :], trans[1, z, at, :]
            if last_chunk:
                t_col = jnp.where(sub == 7, 0.0, t_col)
            t_row = jnp.where(lane == rows - 1, 0.0, t_row)
            col = face_terms(t_col, p - nexts[0], dp - nexts[1])
            row = face_terms(t_row, p - sides[0], dp - sides[1])
            divergence = []
            for a in range(3):
                m, dm = now[z][2 + a], now[z][5 + a]
                flux_col = face_flux(col, m, dm, nexts[2 + a], nexts[5 + a])
                flux_row = face_flux(row, m, dm, sides[2 + a], sides[5 + a])
                both = []
                for t in (0, 1):
                    f, g = flux_col[t], flux_row[t]
                    rolled = pltpu.roll(f, 1, 0)
                    down = jnp.where(sub == 0, before[3 * t + a][z], rolled)
                    before[3 * t + a][z] = rolled
                    both.append(base[3 * t + a, z, at, :] + (f - down) + (g - pltpu.roll(g, 1, 1)))
                divergence.append(both)
            sums.append(divergence)
        for z in range(layers - 1):
            dpot = now[z][1] - now[z + 1][1]
            t_lay = trans[2, z, at, :]
            for a in range(3):
                pot = now[z][0] - now[z + 1][0] + DENSITY[a] * GRAVITY
                terms = face_terms(t_lay, pot, dpot)
                flux = face_flux(
                    terms, now[z][2 + a], now[z][5 + a], now[z + 1][2 + a], now[z + 1][5 + a]
                )
                for t in (0, 1):
                    sums[z][a][t] = sums[z][a][t] + flux[t]
                    sums[z + 1][a][t] = sums[z + 1][a][t] - flux[t]
        for z in range(layers):
            for a in range(3):
                for t in (0, 1):
                    inner[3 * t + a, z, at, :] = sums[z][a][t]
        if not last_chunk:
            now, up = later, up_later
        if c % 2 == 1 and c // 2 < levels:
            for i in range(share):
                reaches[i] = jnp.minimum(dot(reaches[i], reaches[i]), 1.0).astype(BF16)
    for level in range(chunks // 2, levels):
        for i in range(share):
            reaches[i] = jnp.minimum(dot(reaches[i], reaches[i]), 1.0).astype(BF16)
    for i in range(share):
        reach[i] = reaches[i]


def scatter_kernel(
    inner,
    old_mass,
    rates,
    rowloc,
    lxs,
    acc,
    packed,
    active,
):
    layers, cols, rows = acc.shape[1:]
    cells = layers * cols
    wells, segs = rates.shape[1] - 8, rates.shape[2]
    count = list_wells(rowloc[0:wells, :] >= 0, active)
    packed[...] = rates[0, wells + 4 : wells + 4 + packed.shape[0], :]

    for k in range(6):
        acc[k] = inner[k] - old_mass[k] if k < 3 else inner[k]

    sub_row = iota((rows, 4 * segs), 0)
    sub_lx = iota((cells, 4 * segs), 0)

    def scatter_wells(i, carry):
        ids = [active[1 + 4 * i + k] for k in range(4)]
        row = jnp.concatenate([rowloc[pl.ds(w, 1), :] for w in ids], axis=1)
        lx = jnp.concatenate([lxs[pl.ds(w, 1), :] for w in ids], axis=1)
        at = sub_row == row
        hot = jnp.where(sub_lx == lx, 1.0, 0.0).astype(BF16)
        hot = jnp.concatenate([hot, hot], axis=1)
        for q in range(0, 6, 2):
            both = []
            for k in (q, q + 1):
                rate = jnp.concatenate([rates[k, pl.ds(w, 1), :] for w in ids], axis=1)
                terms = [jnp.where(at, term, 0.0).astype(BF16) for term in split(rate, 2)]
                both.append(jnp.concatenate(terms, axis=1))
            part = dot(hot, jnp.concatenate(both, axis=0), NT)
            acc[q] = acc[q] + part[:, 0:rows].reshape(layers, cols, rows)
            acc[q + 1] = acc[q + 1] + part[:, rows : 2 * rows].reshape(layers, cols, rows)
        return carry

    lax.fori_loop(0, (count + 3) // 4, scatter_wells, 0)


def sides_kernel(
    acc, edges, inside_pair, between_pairs, out_hbm, dout_hbm, rims, out, turned, sems
):
    layers, cols, rows = out.shape[1:]
    gy, yi = lax.axis_size("gy"), lax.axis_index("gy")
    even = lax.rem(yi, 2) == 0
    one, other = inside_pair[...], between_pairs[...]
    prev, after = jnp.where(even, other, one), jnp.where(even, one, other)
    flux = outer_flux(edges[2], edges[3], prev, after, yi > 0, yi < gy - 1, layers)
    spare = jnp.zeros((128 - 12 * layers, rows), F32)
    turned[...] = jnp.concatenate(flux + [spare], axis=0).T
    lane = iota((cols, rows), 1)
    moves = []
    for k in range(6):
        for z in range(layers):
            j = 2 * layers * k + z
            before = turned[:, j : j + 1]
            behind = turned[:, j + layers : j + layers + 1]
            side = jnp.where(lane == 0, -before, jnp.where(lane == rows - 1, behind, 0.0))
            out[k, z] = acc[k, z] + side
            rims[k, 0, z] = out[k, z, 0:8, :]
            rims[k, 1, z] = out[k, z, cols - 8 : cols, :]
        final = out_hbm.at[k] if k < 3 else dout_hbm.at[k - 3]
        moves.append(pltpu.make_async_copy(out.at[k], final, sems.at[k]))
        moves[k].start()
    for move in moves:
        move.wait()


def finish_kernel(
    wells,
    out_before,
    dout_before,
    rims,
    reach,
    known,
    packed,
    edges,
    got,
    out_hbm,
    dout_hbm,
    seg_out_hbm,
    seg_dout_hbm,
    group_out_hbm,
    tiles,
    seg_out,
    seg_dout,
    group_out,
    sems,
):
    del out_before, dout_before
    layers = tiles.shape[3]
    cols = out_hbm.shape[2]
    share, segs = seg_out.shape
    gx, gy = lax.axis_size("gx"), lax.axis_size("gy")
    xi, yi = lax.axis_index("gx"), lax.axis_index("gy")
    chunk = got.shape[1]

    has_prev, has_next = xi > 0, xi < gx - 1
    prev, after = (
        got[pl.ds(jnp.where(inside, yi * gx + x, 0), 1), 0 : 7 * layers, :][0]
        for inside, x in ((has_prev, xi - 1), (has_next, xi + 1))
    )
    flux = outer_flux(edges[0], edges[1], prev, after, has_prev, has_next, layers)
    moves = []

    def write(src, dst):
        move = pltpu.make_async_copy(src, dst, sems.at[len(moves)])
        move.start()
        moves.append(move)

    for t, final in ((0, out_hbm), (1, dout_hbm)):
        for side, at in ((0, 0), (1, 7)):
            for a in range(3):
                k = 3 * t + a
                for z in range(layers):
                    tiles[t, side, a, z] = rims[k, side, z]
                    f = flux[k][side * layers + z : side * layers + z + 1]
                    line = rims[k, side, z, at : at + 1, :]
                    tiles[t, side, a, z, at : at + 1, :] = line - f if side == 0 else line + f
            write(tiles.at[t, side], final.at[:, :, pl.ds(side * (cols - 8), 8), :])

    total = got[xi, 0 : 2 * share, :]
    for y in range(1, gy):
        total = total + got[y * gx + xi, 0 : 2 * share, :]

    lines, numbers = [], []
    for x in range(gx):
        line = got[x, chunk - 2 : chunk - 1, :]
        more = line
        for y in range(1, gy):
            more = more + got[y * gx + x, chunk - 2 : chunk - 1, :]
        lines.append(jnp.where(iota((1, 128), 1) < 3 * wells, more, line))
        numbers.append(got[x, chunk - 1 : chunk, :])
    columns = jnp.concatenate(lines + numbers + [jnp.zeros((128 - 2 * gx, 128), F32)], axis=0).T
    group_sums = [jnp.zeros((wells, 128), F32)] * 4
    for x in range(gx):
        member = columns[0:wells, gx + x : gx + x + 1] == iota((wells, 128), 1).astype(F32)
        for a in range(4):
            values = columns[a * wells : (a + 1) * wells, x : x + 1]
            group_sums[a] = group_sums[a] + jnp.where(member, values, 0.0)
    for a in range(3):
        group_out[a : a + 1, :] = jnp.sum(group_sums[a], axis=0, keepdims=True)
    write(group_out, group_out_hbm)
    guide_total = jnp.sum(group_sums[3], axis=0, keepdims=True)

    flows, dflows = [], []
    pad = jnp.zeros((10, segs), F32)
    for i in range(share):
        lines = split(total[i : i + 1], 3) + split(total[share + i : share + i + 1], 3) + [pad]
        flow = dot(jnp.concatenate(lines, axis=0).astype(BF16), reach[i], NT)
        flows.append(flow[0:1] + flow[1:2] + flow[2:3])
        dflows.append(flow[3:4] + flow[4:5] + flow[5:6])
    flow, dflow = jnp.concatenate(flows, axis=0), jnp.concatenate(dflows, axis=0)
    column = [packed[:, k : k + 1] for k in range(5)]
    member = column[2] == iota((share, 128), 1).astype(F32)
    of_group = jnp.sum(jnp.where(member, guide_total, 0.0), axis=1, keepdims=True)
    target = column[3] * column[1] / of_group
    by_rate = column[0] == 1.0
    first = iota((share, segs), 1) == 0
    limit, dlimit = known[0:share, :], known[share : 2 * share, :]
    root = jnp.where(by_rate, RATE_SCALE * (flow - target), limit - column[4])
    droot = jnp.where(by_rate, RATE_SCALE * dflow, dlimit)
    seg_out[...] = jnp.where(first, root, limit - FRICTION * flow)
    seg_dout[...] = jnp.where(first, droot, dlimit - FRICTION * dflow)
    write(seg_out, seg_out_hbm)
    write(seg_dout, seg_dout_hbm)
    for move in moves:
        move.wait()


VMEM = pl.BlockSpec(memory_space=pltpu.VMEM)
ANY = pl.BlockSpec(memory_space=pl.ANY)


def params(mebibytes):
    return pltpu.CompilerParams(vmem_limit_bytes=mebibytes * 1024 * 1024)


def per_device(
    pressure,
    saturations,
    old_mass,
    pore_volume,
    transmissibility,
    direction,
    seg_pressure,
    seg_direction,
    perf_cell,
    well_index,
    parent,
    seg_head,
    well_mode,
    bhp_limit,
    guide_rate,
    group_of,
    group_target,
):
    layers, cols, rows = pressure.shape
    wells, segs = seg_pressure.shape
    cells = layers * cols
    gx, gy = lax.axis_size("gx"), lax.axis_size("gy")
    share = wells // gy
    edge_rows = 7 * layers
    chunk = 2 + max(2 * share, edge_rows)
    shape = jax.ShapeDtypeStruct

    guide_line = guide_rate.reshape(1, wells)
    group_line = group_of.reshape(1, wells)
    send, rates, rowloc, lxs = pl.pallas_call(
        functools.partial(wells_kernel, rows * gy),
        out_shape=(
            shape((gx * gy, chunk, 128), F32),
            shape((6, wells + 8, segs), F32),
            shape((wells + 8, segs), jnp.int32),
            shape((wells + 8, segs), jnp.int32),
        ),
        in_specs=[ANY] * 13,
        out_specs=(VMEM,) * 4,
        scratch_shapes=[
            pltpu.VMEM((wells, segs), jnp.int32),
            pltpu.VMEM((layers, cols, rows), F32),
            pltpu.VMEM((2, layers, cols, rows), F32),
            pltpu.VMEM((3, layers, cols, rows), F32),
            pltpu.VMEM((wells, segs), F32),
            pltpu.VMEM((wells, segs), F32),
            pltpu.VMEM((wells, segs), F32),
            pltpu.VMEM((1, wells), F32),
            pltpu.VMEM((1, wells), jnp.int32),
            pltpu.VMEM((1, wells), jnp.int32),
            pltpu.VMEM((1, wells), F32),
            pltpu.VMEM((1, 128), F32),
            pltpu.VMEM((layers, 8, rows), F32),
            pltpu.VMEM((6, cells, 2 * rows), BF16),
            pltpu.VMEM((cells, rows), BF16),
            pltpu.VMEM((6, wells + 8, segs), F32),
            pltpu.SMEM((wells + 8,), jnp.int32),
            pltpu.SemaphoreType.DMA((13,)),
        ],
        compiler_params=params(56),
        name="wells",
    )(
        perf_cell,
        pressure,
        saturations,
        direction,
        seg_pressure,
        seg_direction,
        well_index,
        guide_line,
        group_line,
        well_mode.reshape(1, wells),
        bhp_limit.reshape(1, wells),
        group_target.reshape(1, 128),
        transmissibility,
    )

    got = lax.all_to_all(send, ("gy", "gx"), 0, 0, tiled=True)

    seg_head, rowloc = lax.optimization_barrier((seg_head, rowloc))

    inner, reach, known, edges, inside_pair, between_pairs = pl.pallas_call(
        cells_kernel,
        out_shape=(
            shape((6, layers, cols, rows), F32),
            shape((share, segs, segs), BF16),
            shape((2 * share, segs), F32),
            shape((4, edge_rows, 128), F32),
            shape((edge_rows, 128), F32),
            shape((edge_rows, 128), F32),
        ),
        in_specs=[VMEM] * 9,
        out_specs=(VMEM,) * 6,
        scratch_shapes=[
            pltpu.VMEM((6, layers, cols, rows), F32),
            pltpu.VMEM((6, layers, cols, rows), F32),
        ],
        compiler_params=params(32),
        cost_estimate=pl.CostEstimate(flops=300_000_000, bytes_accessed=4_000_000, transcendentals=400_000),
        name="cells",
    )(
        pressure,
        saturations,
        pore_volume,
        transmissibility,
        direction,
        parent,
        seg_pressure,
        seg_direction,
        seg_head,
    )

    def swap(x, first):
        pairs = [(i, i + 1) for i in range(first, gy - 1, 2)]
        return lax.ppermute(x, "gy", pairs + [(j, i) for i, j in pairs])

    inside_pair = swap(inside_pair, 0)
    between_pairs = swap(between_pairs, 1)

    cell_shape = shape((3, layers, cols, rows), F32)
    summed, packed = pl.pallas_call(
        scatter_kernel,
        out_shape=(shape((6, layers, cols, rows), F32), shape((share, 128), F32)),
        in_specs=[VMEM] * 5,
        out_specs=(VMEM, VMEM),
        scratch_shapes=[pltpu.SMEM((wells + 8,), jnp.int32)],
        compiler_params=params(32),
        cost_estimate=pl.CostEstimate(flops=300_000_000, bytes_accessed=4_000_000, transcendentals=0),
        name="scatter",
    )(
        inner,
        old_mass,
        rates,
        rowloc,
        lxs,
    )

    out, dout, rims = pl.pallas_call(
        sides_kernel,
        out_shape=(cell_shape, cell_shape, shape((6, 2, layers, 8, rows), F32)),
        in_specs=[VMEM] * 4,
        out_specs=(ANY, ANY, VMEM),
        scratch_shapes=[
            pltpu.VMEM((6, layers, cols, rows), F32),
            pltpu.VMEM((cols, 128), F32),
            pltpu.SemaphoreType.DMA((6,)),
        ],
        compiler_params=params(32),
        cost_estimate=pl.CostEstimate(flops=3_000_000, bytes_accessed=4_000_000, transcendentals=10_000),
        name="sides",
    )(summed, edges, inside_pair, between_pairs)

    out, dout, seg_out, seg_dout, groups = pl.pallas_call(
        functools.partial(finish_kernel, wells),
        out_shape=(
            cell_shape,
            cell_shape,
            shape((share, segs), F32),
            shape((share, segs), F32),
            shape((3, 128), F32),
        ),
        in_specs=[ANY] * 2 + [VMEM] * 6,
        out_specs=(ANY,) * 5,
        input_output_aliases={0: 0, 1: 1},
        scratch_shapes=[
            pltpu.VMEM((2, 2, 3, layers, 8, rows), F32),
            pltpu.VMEM((share, segs), F32),
            pltpu.VMEM((share, segs), F32),
            pltpu.VMEM((3, 128), F32),
            pltpu.SemaphoreType.DMA((7,)),
        ],
        compiler_params=params(32),
        name="finish",
    )(out, dout, rims, reach, known, packed, edges, got)
    return out, dout, seg_out, seg_dout, groups


def solution(mesh):
    placed = (
        P(None, "gx", "gy"),
        P(None, None, "gx", "gy"),
        P(None, None, "gx", "gy"),
        P(None, "gx", "gy"),
        P(None, None, "gx", "gy"),
        P(None, None, "gx", "gy"),
        P("gx", None),
        P("gx", None),
        P("gx", None),
        P("gx", None),
        P("gx", None),
        P("gx", None),
        P("gx"),
        P("gx"),
        P("gx"),
        P("gx", None),
        P(),
    )
    return jax.shard_map(
        per_device,
        mesh=mesh,
        in_specs=placed,
        out_specs=(
            P(None, None, "gx", "gy"),
            P(None, None, "gx", "gy"),
            P(("gx", "gy"), None),
            P(("gx", "gy"), None),
            P(),
        ),
        check_vma=False,
    )
```
